512 devices in a mesh: grp: 8 (over y), tp: 16 (over z, x_lo), rep: 4 (over x_hi, core).
Axes of the slice: x: 4 (x_hi: 2, x_lo: 2; x = x_hi * 2 + x_lo), y: 8, z: 8, core: 2. Of those that a mesh axis runs over, the one named last changes fastest.
Arguments:
- hist: bfloat16 [1024, 4096], P('grp', ('tp', 'rep')), may hold values from -6 to 6
- tower_gain: bfloat16 [1, 4096], P(None, ('tp', 'rep')), may hold values from 0.5 to 1.5
- up_w: bfloat16 [4096, 8192], P(None, ('tp', 'rep')), may hold values from -0.09375 to 0.09375
- down_w: bfloat16 [8192, 4096], P(('tp', 'rep')), may hold values from -0.0625 to 0.0625
- query: bfloat16 [4096], P(('tp', 'rep')), may hold values from -0.19921875 to 0.19921875
- proj_w: bfloat16 [4096, 2048], P(('tp', 'rep')), may hold values from -0.09375 to 0.09375
- cand: bfloat16 [16384, 2048], P(('grp', 'tp', 'rep')), may hold values from -6 to 6
- owner: int32 [16384], P(('grp', 'tp', 'rep')), may hold values from 0 to 4, as said below
- task: int32 [16384], P(('grp', 'tp', 'rep')), may hold values from 0 to 3
- cross_u: bfloat16 [2048, 128], replicated, may hold values from -0.125 to 0.125
- cross_v: bfloat16 [128, 2048], replicated, may hold values from -0.5 to 0.5
- cross_bias: bfloat16 [2048], replicated, may hold values from -3 to 3
- gate_w: bfloat16 [2048, 12], replicated, may hold values from -0.125 to 0.125
- expert_w: bfloat16 [3, 2048, 8192], P(None, None, ('tp', 'rep')), may hold values from -0.125 to 0.125
- head_w: bfloat16 [4, 3, 8192], P(None, None, ('tp', 'rep')), may hold values from -0.0625 to 0.0625
Outputs:
- score: float32 [16384], P(('grp', 'tp', 'rep'))
The draws below stay inside these ranges and needn't reach their ends.
Inputs may be any that keep to these rules, and one draw needn't show every extreme that they name: owner is a request among the 4 of the slot's index of grp, or 4 for an empty slot; on every device the live slots come before the empty ones, and every device has an empty slot.
All inputs are finite; a program needn't handle non-finite values.
Results may differ from the reference program's by a relative error of at most 0.04.
Values may be sent and summed in bfloat16 or wider, within the bound.
No kernel may reach another device: no remote copies, remote signals or barrier semaphores. Data moves between devices by JAX's collectives and lax.ppermute only.
A program may use at most 64 MiB of HBM per device.

```python
import math
import jax
import jax.numpy as jnp
from jax import lax

D = 4096
FF = 8192
E_IN = 2048
E_HID = 8192
RANK = 128
EXPERTS = 3
TASKS = 4
REQ_GRP = 4
HIST = 32
CAND_DEV = 32
REQS = 32
TOKENS = 1024
CAND_ROWS = 16384
N_TP = 16
N_REP = 4


def draw_owner(key, part):
    key = jax.random.fold_in(key, 7)
    count_key, request_key = jax.random.split(key)
    blocks = CAND_ROWS // CAND_DEV
    lowest = max(1, CAND_DEV // 4)
    live_count = jax.random.randint(count_key, (blocks, 1), lowest, CAND_DEV)
    slot_index = jnp.arange(CAND_DEV)[None, :]
    chosen = jax.random.randint(request_key, (blocks, CAND_DEV), 0, REQ_GRP)
    return jnp.where(slot_index < live_count, chosen, REQ_GRP).reshape(CAND_ROWS).astype(jnp.int32)


def place_ends(drawn, rng, least, high):
    dims = drawn.shape
    index_at = [jax.random.randint(jax.random.fold_in(rng, axis), (), 0, dims[axis]) for axis in range(len(dims))]
    drawn = drawn.at[tuple(index_at)].set(least)
    longest = dims.index(max(dims))
    index_at[longest] = (index_at[longest] + 1) % dims[longest]
    return drawn.at[tuple(index_at)].set(high)


def level_of(rng, dims, cuts, smallest, largest):
    factor_of = 1.0
    for dim, blocks in cuts:
        steps = jax.random.uniform(jax.random.fold_in(jax.random.fold_in(rng, 6), dim), (blocks,), jnp.float32, smallest / len(cuts), largest / len(cuts))
        factor_of = factor_of * jnp.repeat(jnp.exp(steps), dims[dim] // blocks).reshape((-1,) + (1,) * (len(dims) - 1 - dim))
    return factor_of


def normal_values(rng, dims, scale, bound, pieces=(), kind=jnp.bfloat16):
    values = jax.random.normal(rng, dims, jnp.float32) * scale
    if len(pieces) > 0:
        values = level_of(rng, dims, pieces, -0.22, 0.18) * values
    return jnp.clip(values, min=-bound, max=bound).astype(kind)


def setup_inputs(seed: int = 0) -> dict:
    splits = jax.random.split(jax.random.key(seed), 16)
    return {
        "hist": normal_values(splits[0], (TOKENS, D), 1.0, 6.0, ((0, 8), (1, 64))),
        "tower_gain": jnp.clip(1.0 + 0.1 * jax.random.normal(splits[1], (1, D), jnp.float32), 0.5, 1.5).astype(jnp.bfloat16),
        "up_w": normal_values(splits[2], (D, FF), D ** -0.5, 0.09375, ((1, 64),)),
        "down_w": normal_values(splits[3], (FF, D), FF ** -0.5, 0.0625, ((0, 64),)),
        "query": normal_values(splits[4], (D,), 0.03, 0.19921875, ((0, 64),)),
        "proj_w": normal_values(splits[5], (D, E_IN), D ** -0.5, 0.09375, ((0, 64),)),
        "cand": normal_values(splits[6], (CAND_ROWS, E_IN), 1.0, 6.0, ((0, 512),)),
        "owner": draw_owner(jax.random.fold_in(splits[15], 71), 0),
        "task": place_ends(jax.random.randint(splits[8], (CAND_ROWS,), 0, TASKS), jax.random.fold_in(splits[8], 1), 0, TASKS - 1).astype(jnp.int32),
        "cross_u": normal_values(splits[9], (E_IN, RANK), E_IN ** -0.5, 0.125),
        "cross_v": normal_values(splits[10], (RANK, E_IN), RANK ** -0.5, 0.5),
        "cross_bias": normal_values(splits[11], (E_IN,), 0.5, 3.0),
        "gate_w": normal_values(splits[12], (E_IN, TASKS * EXPERTS), E_IN ** -0.5, 0.125),
        "expert_w": normal_values(splits[13], (EXPERTS, E_IN, E_HID), E_IN ** -0.5, 0.125, ((2, 64),)),
        "head_w": normal_values(splits[14], (TASKS, EXPERTS, E_HID), E_HID ** -0.5, 0.0625, ((2, 64),)),
    }


epsilon = 1e-05

def reference(hist, tower_gain, up_w, down_w, query, proj_w, cand, owner, task, cross_u, cross_v, cross_bias, gate_w, expert_w, head_w):
    hist_f = hist.astype(jnp.float32)
    scaled = (hist_f * tower_gain.astype(jnp.float32)).astype(jnp.bfloat16)
    inverse = lax.rsqrt(lax.optimization_barrier(jnp.mean(hist_f * hist_f, axis=1, keepdims=True)) + epsilon)
    hidden = jax.nn.gelu(jnp.dot(scaled, up_w, preferred_element_type=jnp.float32) * inverse).astype(jnp.bfloat16)
    tower_out = (hist_f + jnp.dot(hidden, down_w, preferred_element_type=jnp.float32)).astype(jnp.bfloat16)
    out_f = tower_out.astype(jnp.float32)
    dotted = lax.optimization_barrier(jnp.sum(out_f * query.astype(jnp.float32)[None, :], axis=1))
    weight = jax.nn.sigmoid(dotted * lax.rsqrt(lax.optimization_barrier(jnp.mean(out_f * out_f, axis=1)) + epsilon))
    values = jnp.dot(tower_out, proj_w, preferred_element_type=jnp.float32)
    user = lax.optimization_barrier(jnp.sum((weight[:, None] * values).reshape(REQS, HIST, E_IN), axis=1)) / math.sqrt(HIST)
    block_of = (jnp.arange(CAND_ROWS) // (CAND_DEV * N_TP * N_REP)).astype(jnp.int32)
    live = owner < REQ_GRP
    request = (block_of * REQ_GRP + jnp.minimum(owner, REQ_GRP - 1)).astype(jnp.int32)
    added = jnp.where(live[:, None], user[request], jnp.float32(0.0))
    x0 = (cand.astype(jnp.float32) + added).astype(jnp.bfloat16)
    low = jnp.dot(x0, cross_u, preferred_element_type=jnp.float32).astype(jnp.bfloat16)
    x0_f = x0.astype(jnp.float32)
    cross = jnp.dot(low, cross_v, preferred_element_type=jnp.float32) + cross_bias.astype(jnp.float32)[None, :]
    x1 = (x0_f * cross + x0_f).astype(jnp.bfloat16)
    task_hot = (task[:, None] == jnp.arange(TASKS).astype(jnp.int32)[None, :]).astype(jnp.float32)
    logits = jnp.dot(x1, gate_w, preferred_element_type=jnp.float32).reshape(CAND_ROWS, TASKS, EXPERTS)
    picked = jax.nn.sigmoid(lax.optimization_barrier(jnp.sum(logits * task_hot[:, :, None], axis=1)))
    gates = picked / lax.optimization_barrier(jnp.sum(picked, axis=1, keepdims=True))

    def one_expert(pair):
        weights, heads = pair
        active = jax.nn.relu(jnp.dot(x1, weights, preferred_element_type=jnp.float32)).astype(jnp.bfloat16)
        return jnp.dot(active, heads.T, preferred_element_type=jnp.float32)
    per_expert = lax.map(one_expert, (expert_w, jnp.moveaxis(head_w, 1, 0)))
    expert_out = lax.optimization_barrier(jnp.sum(per_expert * task_hot[None, :, :], axis=2)).T
    score = lax.optimization_barrier(jnp.sum(gates * expert_out, axis=1))
    return jnp.where(live, score, jnp.float32(0.0))
```

```python
import math

import jax
import jax.numpy as jnp
from jax import lax
from jax.experimental import pallas as pl
from jax.experimental.pallas import tpu as pltpu
from jax.sharding import Mesh, PartitionSpec as P

D = 4096
EXPERTS = 3
TASKS = 4
REQ_GRP = 4
HIST = 32
epsilon = 1e-05

CHIPS = ("z", "xh", "xl")
ALL = ("z", "xh", "xl", "c")
N_CHIPS = 32
F32 = jnp.float32
BF16 = jnp.bfloat16
HIGH = lax.Precision.HIGHEST

VMEM = pl.BlockSpec(memory_space=pltpu.VMEM)


def params(mib):
    return pltpu.CompilerParams(vmem_limit_bytes=mib << 20)


def block_of(chip):
    return (chip & ~3) | ((chip & 1) << 1) | ((chip >> 1) & 1)


def split2(x):
    high = x.astype(BF16).astype(F32)
    return high, x - high


def lanes(shape):
    return lax.broadcasted_iota(jnp.int32, shape, len(shape) - 1)


def rows(shape):
    return lax.broadcasted_iota(jnp.int32, shape, len(shape) - 2)


def token_sums(x):
    padded = jnp.concatenate([x, jnp.zeros_like(x)], axis=0)
    return lax.dot_general(
        jnp.ones((16, 128), F32), padded, (((1,), (1,)), ((), ())), precision=HIGH, preferred_element_type=F32
    )


def spread_kernel(pair_ref, slots_ref, out_ref, hist_ref, query_ref):
    core = lax.axis_index("c")
    tokens = pl.ds(pl.multiple_of(core * 64, 64), 64)
    first = pair_ref[0, tokens, :].astype(F32)
    second = pair_ref[1, tokens, :].astype(F32)
    low = lanes((64, 128)) < 64
    hist = jnp.where(low, first, pltpu.roll(second, 64, 1))
    head0 = pair_ref[0, 128:144, :].astype(F32)[0:1]
    head1 = pair_ref[1, 128:144, :].astype(F32)[0:1]
    low1 = lanes((1, 128)) < 64
    gain = jnp.where(low1, head0, pltpu.roll(jnp.broadcast_to(head1, (8, 128)), 64, 1)[0:1])
    query = jnp.where(low1, pltpu.roll(jnp.broadcast_to(head0, (8, 128)), 64, 1)[0:1], head1)
    scaled = (hist * gain).astype(BF16)
    high, rest = split2(token_sums(hist * hist))
    owner = slots_ref[0:1, :].astype(F32)
    task = slots_ref[1:2, :].astype(F32)
    row = rows((16, 128))
    extra = jnp.where(row == 0, high, jnp.where(row == 1, rest, jnp.where(row == 2, owner, jnp.where(row == 3, task, 0.0))))
    extra = extra.astype(BF16)
    for chip in range(N_CHIPS):
        out_ref[chip, 0:64, :] = scaled
        out_ref[chip, 64:80, :] = extra
    hist_ref[...] = hist.astype(BF16)
    query_ref[...] = jnp.broadcast_to(query, (8, 128))


def tower_kernel(got_ref, up0_ref, up1_ref, down0_ref, down1_ref, out_ref, owner_ref, task_ref):
    stats = jnp.zeros((16, 128), F32)
    extras = []
    for chip in range(N_CHIPS):
        extra = got_ref[chip, 64:80, :].astype(F32)
        stats = stats + extra
        extras.append(extra)
    quarter = lanes((1, 128)) // 32
    owners, tasks = [], []
    for b in range(8):
        owner = jnp.zeros((1, 128), F32)
        task = jnp.zeros((1, 128), F32)
        for q in range(4):
            owner = jnp.where(quarter == q, extras[4 * b + q][2:3], owner)
            task = jnp.where(quarter == q, extras[4 * b + q][3:4], task)
        owners.append(owner)
        tasks.append(task)
    owner_ref[...] = jnp.concatenate(owners, axis=0)
    task_ref[...] = jnp.concatenate(tasks, axis=0)
    inverse = lax.rsqrt((stats[0:1] + stats[1:2]) / D + epsilon)
    column = jnp.broadcast_to(inverse, (128, 128)).T[0:64]
    total = jnp.zeros((64, 256), F32)
    for b in range(0, N_CHIPS, 2):
        left = jnp.concatenate([got_ref[block_of(b), 0:64, :], got_ref[block_of(b + 1), 0:64, :]], axis=1)
        right = jnp.concatenate([up0_ref[b * 128 : b * 128 + 256, :], up1_ref[b * 128 : b * 128 + 256, :]], axis=1)
        total = total + jnp.dot(left, right, preferred_element_type=F32)
    hidden = jax.nn.gelu(total * jnp.concatenate([column, column], axis=1)).astype(BF16)
    for b in range(0, N_CHIPS, 2):
        right = jnp.concatenate([down0_ref[:, b * 128 : b * 128 + 256], down1_ref[:, b * 128 : b * 128 + 256]], axis=0)
        part = jnp.dot(hidden, right, preferred_element_type=F32).astype(BF16)
        out_ref[block_of(b), :, :] = part[:, 0:128]
        out_ref[block_of(b + 1), :, :] = part[:, 128:256]


def values_kernel(got_ref, hist_ref, query_ref, proj0_ref, proj1_ref, out_ref):
    core = lax.axis_index("c")
    summed = got_ref[0].astype(F32)
    for chip in range(1, N_CHIPS):
        summed = summed + got_ref[chip].astype(F32)
    tower = (hist_ref[...].astype(F32) + summed).astype(BF16).astype(F32)
    square_high, square_rest = split2(token_sums(tower * tower))
    dot_high, dot_rest = split2(token_sums(tower * query_ref[0:1, :]))
    row = rows((16, 128))
    extra = jnp.where(
        row == 0, square_high, jnp.where(row == 1, square_rest, jnp.where(row == 2, dot_high, jnp.where(row == 3, dot_rest, 0.0)))
    ).astype(BF16)
    mine = jnp.where(core == 0, tower, pltpu.roll(tower, 64, 1)).astype(BF16)
    low = lanes((32, 128)) < 64
    for j in range(16):
        cols = slice(128 * j, 128 * j + 128)
        right = jnp.concatenate([proj0_ref[:, cols], proj1_ref[:, cols]], axis=0)
        part = jnp.dot(mine, right, preferred_element_type=F32)
        turned = pltpu.roll(part, 64, 1)
        out_ref[2 * j, 0:32, :] = jnp.where(low, part[0:32], turned[32:64]).astype(BF16)
        out_ref[2 * j + 1, 0:32, :] = jnp.where(low, turned[0:32], part[32:64]).astype(BF16)
        out_ref[2 * j, 32:48, :] = extra
        out_ref[2 * j + 1, 32:48, :] = extra


def user_kernel(got_ref, out_ref):
    values = got_ref[0].astype(F32)
    for chip in range(1, N_CHIPS):
        values = values + got_ref[chip].astype(F32)
    stats = values[32:48]
    squares = stats[0:1] + stats[1:2]
    dotted = stats[2:3] + stats[3:4]
    weight = jax.nn.sigmoid(dotted * lax.rsqrt(squares / D + epsilon))
    column = jnp.broadcast_to(weight, (128, 128)).T
    weights = jnp.where(lanes((32, 128)) < 64, column[0:32], column[32:64])
    user = jnp.sum(weights * values[0:32], axis=0, keepdims=True) / math.sqrt(HIST)
    out_ref[...] = jnp.broadcast_to(user, (64, 128))


ROWS = 256


def score_kernel(
    user_ref, cand_ref, owner_ref, task_ref, pair_ref, cross_u_ref, cross_v_ref, bias_ref, gate_ref, w0_ref, w1_ref,
    out_ref, users, x0s, x1s,
):
    core = lax.axis_index("c")
    step = pl.program_id(0)

    @pl.when(step == 0)
    def _():
        got = user_ref[...]
        turned = pltpu.roll(got, 64, 1)
        row = rows((16, 128))
        low = lanes((1, 128)) < 64
        for j in range(16):
            a = 4 * j
            picks = []
            for c in range(2):
                picks.append(jnp.where(low, got[a + c : a + c + 1], turned[a + 2 + c : a + 3 + c]))
                picks.append(jnp.where(low, turned[a + c : a + c + 1], got[a + 2 + c : a + 3 + c]))
            r4 = row % 4
            full = jnp.where(r4 == 0, picks[0], jnp.where(r4 == 1, picks[1], jnp.where(r4 == 2, picks[2], picks[3])))
            high, rest = split2(full)
            mid, last = split2(rest)
            users[:, 128 * j : 128 * j + 128] = jnp.where(
                row < 4, high, jnp.where(row < 8, mid, jnp.where(row < 12, last, 0.0))
            ).astype(BF16)

    owner = jnp.concatenate([owner_ref[pl.ds(2 * step, 1), :], owner_ref[pl.ds(2 * step + 1, 1), :]], axis=1)
    task = jnp.concatenate([task_ref[pl.ds(2 * step, 1), :], task_ref[pl.ds(2 * step + 1, 1), :]], axis=1)
    row = rows((16, ROWS))
    hot = jnp.where((row % 4).astype(F32) == owner, 1.0, 0.0)
    hot = hot.T.astype(BF16)
    low = jnp.zeros((ROWS, 128), F32)
    for j in range(8):
        cols = slice(256 * j, 256 * j + 256)
        added = jnp.dot(hot, users[:, cols], preferred_element_type=F32)
        x0 = (cand_ref[:, cols].astype(F32) + added).astype(BF16)
        x0s[:, cols] = x0
        low = low + jnp.dot(x0, cross_u_ref[cols, :], preferred_element_type=F32)
    low = low.astype(BF16)
    for j in range(8):
        cols = slice(256 * j, 256 * j + 256)
        cross = jnp.dot(low, cross_v_ref[:, cols], preferred_element_type=F32) + bias_ref[:, cols].astype(F32)
        x0 = x0s[:, cols].astype(F32)
        x1s[:, cols] = (x0 * cross + x0).astype(BF16)
    contract = (((1,), (1,)), ((), ()))
    logits = lax.dot_general(gate_ref[...], x1s[...], contract, preferred_element_type=F32)
    heads = jnp.concatenate([pair_ref[core, 144:160, :], pair_ref[1 - core, 144:160, :]], axis=1)
    terms = []
    for k in range(EXPERTS):
        total = jnp.zeros((ROWS, 256), F32)
        for j in range(8):
            cols = slice(256 * j, 256 * j + 256)
            right = jnp.concatenate([w0_ref[k, cols, :], w1_ref[k, cols, :]], axis=1)
            total = total + jnp.dot(x1s[:, cols], right, preferred_element_type=F32)
        active = jax.nn.relu(total).astype(BF16)
        terms.append(lax.dot_general(heads, active, contract, preferred_element_type=F32))
    mine = (row // 3).astype(F32) == task
    picked = jnp.where(mine, jax.nn.sigmoid(logits), 0.0)
    term = jnp.where(row % 3 == 0, terms[0], jnp.where(row % 3 == 1, terms[1], terms[2]))
    gates = picked / jnp.sum(picked, axis=0, keepdims=True)
    part = jnp.sum(jnp.where(mine, gates * term, 0.0), axis=0, keepdims=True)
    for half in range(2):
        out_ref[4 * half : 4 * half + 4, :] = jnp.broadcast_to(part[:, 128 * half : 128 * half + 128], (4, 128))


def home_kernel(got_ref, slots_ref, out_ref):
    place = lax.axis_index("xh") * 2 + lax.axis_index("xl")
    total = jnp.sum(got_ref[...], axis=0, keepdims=True)
    lane = lanes((1, 128))
    quarters = [total] + [pltpu.roll(jnp.broadcast_to(total, (8, 128)), 128 - 32 * q, 1)[0:1] for q in range(1, 4)]
    mine = jnp.where(place == 0, quarters[0], jnp.where(place == 1, quarters[1], jnp.where(place == 2, quarters[2], quarters[3])))
    out_ref[...] = jnp.where(slots_ref[0:1, :] < REQ_GRP, mine, 0.0)


def body(
    hist, tower_gain, up_w, down_w, query, proj_w, cand, owner, task, cross_u, cross_v, cross_bias, gate_w, expert_w, head_w,
):
    everyone = lax.all_gather(cand, CHIPS, axis=0, tiled=True)
    swap = lambda x: lax.ppermute(x, "c", [(0, 1), (1, 0)])
    ends = jnp.concatenate([tower_gain, query[None, :]], axis=1)
    message = jnp.concatenate(
        [jnp.pad(hist, ((0, 0), (0, 64))), jnp.pad(ends, ((0, 15), (0, 0))), jnp.pad(head_w.reshape(12, 128), ((0, 4), (0, 0)))],
        axis=0,
    )
    pair = lax.all_gather(message, "c", axis=0)
    up_other = swap(up_w)
    down_other = swap(down_w)
    slots = jnp.concatenate([jnp.tile(owner[None, :], (1, 4)), jnp.tile(task[None, :], (1, 4))], axis=0)
    spread, hist_c, query_c = pl.pallas_call(
        spread_kernel,
        out_shape=(
            jax.ShapeDtypeStruct((N_CHIPS, 80, 128), BF16),
            jax.ShapeDtypeStruct((64, 128), BF16),
            jax.ShapeDtypeStruct((8, 128), F32),
        ),
        in_specs=[VMEM] * 2,
        out_specs=(VMEM,) * 3,
        compiler_params=params(8),
    )(pair, slots)
    tokens = lax.all_to_all(spread, CHIPS, 0, 0, tiled=True)
    proj_other = swap(proj_w)
    expert_other = swap(expert_w)
    parts, owners, tasks = pl.pallas_call(
        tower_kernel,
        out_shape=(
            jax.ShapeDtypeStruct((N_CHIPS, 64, 128), BF16),
            jax.ShapeDtypeStruct((8, 128), F32),
            jax.ShapeDtypeStruct((8, 128), F32),
        ),
        in_specs=[VMEM] * 5,
        out_specs=(VMEM,) * 3,
        compiler_params=params(16),
    )(tokens, up_w, up_other, down_w, down_other)
    summed = lax.all_to_all(parts, CHIPS, 0, 0, tiled=True)
    values = pl.pallas_call(
        values_kernel,
        out_shape=jax.ShapeDtypeStruct((N_CHIPS, 48, 128), BF16),
        in_specs=[VMEM] * 5,
        out_specs=VMEM,
        compiler_params=params(8),
    )(summed, hist_c, query_c, proj_w, proj_other)
    values = lax.all_to_all(values, CHIPS, 0, 0, tiled=True)
    user = pl.pallas_call(
        user_kernel,
        out_shape=jax.ShapeDtypeStruct((64, 128), F32),
        in_specs=[VMEM],
        out_specs=VMEM,
        compiler_params=params(8),
    )(values)
    users = lax.all_to_all(user, ALL, 0, 0, tiled=True)
    gates = jnp.pad(gate_w.T, ((0, 4), (0, 0)))
    whole = lambda *shape: pl.BlockSpec(shape, lambda i: (0,) * len(shape))
    part = pl.pallas_call(
        score_kernel,
        grid=(4,),
        out_shape=jax.ShapeDtypeStruct((N_CHIPS, 128), F32),
        in_specs=[
            whole(64, 128),
            pl.BlockSpec((ROWS, 2048), lambda i: (i, 0)),
            whole(8, 128),
            whole(8, 128),
            whole(2, 160, 128),
            whole(2048, 128),
            whole(128, 2048),
            whole(1, 2048),
            whole(16, 2048),
            whole(3, 2048, 128),
            whole(3, 2048, 128),
        ],
        out_specs=pl.BlockSpec((8, 128), lambda i: (i, 0)),
        scratch_shapes=[
            pltpu.VMEM((16, 2048), BF16),
            pltpu.VMEM((ROWS, 2048), BF16),
            pltpu.VMEM((ROWS, 2048), BF16),
        ],
        compiler_params=params(32),
    )(users, everyone, owners, tasks, pair, cross_u, cross_v, cross_bias[None, :], gates, expert_w, expert_other)
    back = lax.all_to_all(part, CHIPS, 0, 0, tiled=True)
    score = pl.pallas_call(
        home_kernel,
        out_shape=jax.ShapeDtypeStruct((1, 128), F32),
        in_specs=[VMEM] * 2,
        out_specs=VMEM,
        compiler_params=params(4),
    )(back, slots)
    return score[0, 0:32]


def solution(mesh):
    fine = Mesh(mesh.devices.reshape(mesh.devices.shape[0], 8, 2, 2, 2), ("grp", "z", "xl", "xh", "c"))
    t = ("z", "xl", "xh", "c")
    in_specs = (
        P("grp", t),
        P(None, t),
        P(None, t),
        P(t, None),
        P(t),
        P(t, None),
        P(("grp",) + t, None),
        P(("grp",) + t),
        P(("grp",) + t),
        P(),
        P(),
        P(),
        P(),
        P(None, None, t),
        P(None, None, t),
    )
    return jax.shard_map(body, mesh=fine, in_specs=in_specs, out_specs=P(("grp",) + t), check_vma=False)
```

```python
import math

import jax
import jax.numpy as jnp
from jax import lax
from jax.experimental import pallas as pl
from jax.experimental.pallas import tpu as pltpu
from jax.sharding import Mesh, PartitionSpec as P

D = 4096
EXPERTS = 3
TASKS = 4
REQ_GRP = 4
HIST = 32
epsilon = 1e-05

CHIPS = ("z", "xh", "xl")
ALL = ("z", "xh", "xl", "c")
N_CHIPS = 32
F32 = jnp.float32
BF16 = jnp.bfloat16
HIGH = lax.Precision.HIGHEST

VMEM = pl.BlockSpec(memory_space=pltpu.VMEM)
ANY = pl.BlockSpec(memory_space=pl.ANY)
HBM = pl.BlockSpec(memory_space=pltpu.HBM)
ROW_BY_ROW = (((1,), (1,)), ((), ()))


def params(room_kib):
    return pltpu.CompilerParams(vmem_limit_bytes=(64 << 20) - (room_kib << 10))


def block_of(chip):
    return (chip & ~3) | ((chip & 1) << 1) | ((chip >> 1) & 1)


def split2(x):
    high = x.astype(BF16).astype(F32)
    return high, x - high


def lanes(shape):
    return lax.broadcasted_iota(jnp.int32, shape, len(shape) - 1)


def rows(shape):
    return lax.broadcasted_iota(jnp.int32, shape, len(shape) - 2)


def token_sums(x):
    padded = jnp.concatenate([x, jnp.zeros((128 - x.shape[0], 128), F32)], axis=0)
    return lax.dot_general(jnp.ones((8, 128), F32), padded, ROW_BY_ROW, precision=HIGH, preferred_element_type=F32)


def turn(x, by):
    return pltpu.roll(jnp.broadcast_to(x, (8, 128)), by, 1)[0:1]


def widen(x):
    return jnp.concatenate([x, jnp.zeros((1, 128 - x.shape[1]), x.dtype)], axis=1)


def pack_kernel(hist_ref, gain_ref, query_ref, head_ref, out_ref):
    hist = hist_ref[...].astype(F32)
    out_ref[0:128, :] = jnp.concatenate([hist, jnp.zeros((64, 128), F32)], axis=0).T.astype(BF16)
    row = rows((16, 128))
    ends = jnp.concatenate([gain_ref[...].astype(F32), query_ref[...].astype(F32)], axis=1)
    out_ref[128:144, :] = jnp.where(row == 0, ends, 0.0).astype(BF16)
    heads = jnp.zeros((16, 128), F32)
    for k in range(EXPERTS):
        head = head_ref[k].astype(F32)
        for t in range(TASKS):
            heads = jnp.where(row == t * EXPERTS + k, head[t : t + 1], heads)
    out_ref[144:160, :] = heads.astype(BF16)


def spread_kernel(pair_ref, owner_ref, task_ref, out_ref, hist_ref, query_ref):
    core = lax.axis_index("c")
    tokens = pl.ds(pl.multiple_of(core * 64, 64), 64)
    first = pair_ref[0, tokens, :].astype(F32)
    second = pair_ref[1, tokens, :].astype(F32)
    hist = jnp.where(lanes((64, 128)) < 64, first, pltpu.roll(second, 64, 1))
    head0 = pair_ref[0, 128:144, :].astype(F32)[0:1]
    head1 = pair_ref[1, 128:144, :].astype(F32)[0:1]
    low = lanes((1, 128)) < 64
    gain = jnp.where(low, head0, turn(head1, 64))
    query = jnp.where(low, turn(head0, 64), head1)
    scaled = (hist * gain).astype(BF16)
    high, rest = split2(token_sums(hist * hist))
    owner = widen(owner_ref[...].astype(F32))
    task = widen(task_ref[...].astype(F32))
    owner = owner + turn(owner, 32)
    owner = owner + turn(owner, 64)
    task = task + turn(task, 32)
    task = task + turn(task, 64)
    row = rows((8, 128))
    extra = jnp.where(row == 0, high, jnp.where(row == 1, rest, jnp.where(row == 2, owner, jnp.where(row == 3, task, 0.0))))
    extra = extra.astype(BF16)
    for chip in range(N_CHIPS):
        out_ref[chip, 0:64, :] = scaled
        out_ref[chip, 64:72, :] = extra
    hist_ref[...] = hist.astype(BF16)
    query_ref[...] = jnp.broadcast_to(query, (8, 128))


def piece_chip(piece, z):
    x = lax.axis_index("xh") * 2 + lax.axis_index("xl")
    return z * 4 + ((x + (0, 3, 1, 2)[piece]) & 3)


def tower_kernel(got_ref, up0_ref, up1_ref, down0_ref, down1_ref, out_ref, owner_ref, task_ref, up, down, sems):
    copies = []
    for i, source in enumerate((up0_ref, up1_ref)):
        copies.append(pltpu.make_async_copy(source, up.at[i], sems.at[i]))
    for i, source in enumerate((down0_ref, down1_ref)):
        copies.append(pltpu.make_async_copy(source, down.at[i], sems.at[2 + i]))
    for copy in copies:
        copy.start()
    stats = jnp.zeros((8, 128), F32)
    for chip in range(N_CHIPS):
        stats = stats + got_ref[chip, 64:72, :].astype(F32)
    quarter = lanes((1, 128)) // 32
    owners, tasks = [], []
    for b in range(8):
        owner = jnp.zeros((1, 128), F32)
        task = jnp.zeros((1, 128), F32)
        for q in range(4):
            extra = got_ref[piece_chip(b // 2, 4 * (b % 2) + q), 64:72, :].astype(F32)
            owner = jnp.where(quarter == q, extra[2:3], owner)
            task = jnp.where(quarter == q, extra[3:4], task)
        owners.append(owner)
        tasks.append(task)
    owner_ref[...] = jnp.concatenate(owners, axis=0)
    task_ref[...] = jnp.concatenate(tasks, axis=0)
    inverse = lax.rsqrt((stats[0:1] + stats[1:2]) / D + epsilon)
    column = jnp.broadcast_to(inverse, (128, 128)).T[0:64]
    copies[0].wait()
    copies[1].wait()
    total = jnp.zeros((64, 256), F32)
    for b in range(0, N_CHIPS, 2):
        left = jnp.concatenate([got_ref[block_of(b), 0:64, :], got_ref[block_of(b + 1), 0:64, :]], axis=1)
        right = jnp.concatenate([up[0, b * 128 : b * 128 + 256, :], up[1, b * 128 : b * 128 + 256, :]], axis=1)
        total = total + jnp.dot(left, right, preferred_element_type=F32)
    hidden = jax.nn.gelu(total * jnp.concatenate([column, column], axis=1)).astype(BF16)
    copies[2].wait()
    copies[3].wait()
    for b in range(0, N_CHIPS, 2):
        right = jnp.concatenate([down[0, :, b * 128 : b * 128 + 256], down[1, :, b * 128 : b * 128 + 256]], axis=0)
        part = jnp.dot(hidden, right, preferred_element_type=F32).astype(BF16)
        out_ref[block_of(b), :, :] = part[:, 0:128]
        out_ref[block_of(b + 1), :, :] = part[:, 128:256]


def values_kernel(got_ref, hist_ref, query_ref, proj0_ref, proj1_ref, out_ref, proj, sems):
    copies = []
    for i, source in enumerate((proj0_ref, proj1_ref)):
        copies.append(pltpu.make_async_copy(source, proj.at[64 * i : 64 * i + 64, :], sems.at[i]))
    for copy in copies:
        copy.start()
    core = lax.axis_index("c")
    summed = got_ref[0].astype(F32)
    for chip in range(1, N_CHIPS):
        summed = summed + got_ref[chip].astype(F32)
    tower = (hist_ref[...].astype(F32) + summed).astype(BF16).astype(F32)
    square_high, square_rest = split2(token_sums(tower * tower))
    dot_high, dot_rest = split2(token_sums(tower * query_ref[0:1, :]))
    row = rows((8, 128))
    extra = jnp.where(row == 2, dot_high, jnp.where(row == 3, dot_rest, 0.0))
    extra = jnp.where(row == 0, square_high, jnp.where(row == 1, square_rest, extra)).astype(BF16)
    mine = jnp.where(core == 0, tower, pltpu.roll(tower, 64, 1)).astype(BF16)
    low = lanes((32, 128)) < 64
    for copy in copies:
        copy.wait()
    for j in range(16):
        part = jnp.dot(mine, proj[:, 128 * j : 128 * j + 128], preferred_element_type=F32)
        turned = pltpu.roll(part, 64, 1)
        out_ref[2 * j, 0:32, :] = jnp.where(low, part[0:32], turned[32:64]).astype(BF16)
        out_ref[2 * j + 1, 0:32, :] = jnp.where(low, turned[0:32], part[32:64]).astype(BF16)
        out_ref[2 * j, 32:40, :] = extra
        out_ref[2 * j + 1, 32:40, :] = extra


def user_kernel(got_ref, out_ref):
    values = got_ref[0, 0:32, :].astype(F32)
    stats = got_ref[0, 32:40, :].astype(F32)
    for chip in range(1, N_CHIPS):
        values = values + got_ref[chip, 0:32, :].astype(F32)
        stats = stats + got_ref[chip, 32:40, :].astype(F32)
    squares = stats[0:1] + stats[1:2]
    dotted = stats[2:3] + stats[3:4]
    weight = jax.nn.sigmoid(dotted * lax.rsqrt(squares / D + epsilon))
    column = jnp.broadcast_to(weight, (128, 128)).T
    weights = jnp.where(lanes((32, 128)) < 64, column[0:32], column[32:64])
    user = jnp.sum(weights * values, axis=0, keepdims=True) / math.sqrt(HIST)
    out_ref[...] = jnp.broadcast_to(user, (64, 128))


PIECE = 256


def score_kernel(
    user_ref, c0_ref, c1_ref, c2_ref, c3_ref, c4_ref, owner_ref, task_ref, own_task_ref, pair_ref, cross_u_ref,
    cross_v_ref, bias_ref, gate_ref, w0_ref, w1_ref,
    out_ref, gates_ref, users, x, cross_u, cross_v, w, sems,
):
    core = lax.axis_index("c")
    arrivals = []
    for i, (source, start, size) in enumerate(
        ((c0_ref, 0, 256), (c1_ref, 256, 256), (c2_ref, 512, 256), (c3_ref, 768, 128), (c4_ref, 896, 128))
    ):
        arrivals.append(pltpu.make_async_copy(source, x.at[start : start + size, :], sems.at[i]))
    get_u = pltpu.make_async_copy(cross_u_ref, cross_u, sems.at[5])
    get_v = pltpu.make_async_copy(cross_v_ref, cross_v.at[0:128, :], sems.at[6])
    get_w = [
        pltpu.make_async_copy(w0_ref, w.at[0], sems.at[7]),
        pltpu.make_async_copy(w1_ref, w.at[1], sems.at[8]),
    ]
    for copy in (arrivals[0], get_u, get_v, arrivals[1], *get_w, *arrivals[2:]):
        copy.start()
    got = user_ref[...]
    turned = pltpu.roll(got, 64, 1)
    row = rows((16, 128))
    low_half = lanes((1, 128)) < 64
    for j in range(16):
        full = jnp.zeros((16, 128), F32)
        for r in range(REQ_GRP):
            a = 4 * j + r // 2
            if r % 2 == 0:
                pick = jnp.where(low_half, got[a : a + 1], turned[a + 2 : a + 3])
            else:
                pick = jnp.where(low_half, turned[a : a + 1], got[a + 2 : a + 3])
            full = jnp.where(row % 4 == r, pick, full)
        high, rest = split2(full)
        mid, last = split2(rest)
        users[:, 128 * j : 128 * j + 128] = jnp.where(
            row < 4, high, jnp.where(row < 8, mid, jnp.where(row < 12, last, 0.0))
        ).astype(BF16)
    heads = jnp.concatenate([pair_ref[core, 144:160, :], pair_ref[1 - core, 144:160, :]], axis=1)
    row = rows((16, 2048))
    bias = bias_ref[...].astype(F32)
    cross_v[128:144, :] = jnp.where(row == 0, bias, jnp.where(row == 1, 1.0, 0.0)).astype(BF16)
    cross_v[144:256, :] = jnp.zeros((112, 2048), BF16)
    ones = jnp.where(lanes((PIECE, 128)) < 2, 1.0, 0.0).astype(BF16)
    row = rows((16, PIECE))
    task_row = lambda p, ref: jnp.concatenate([ref[2 * p : 2 * p + 1, :], ref[2 * p + 1 : 2 * p + 2, :]], axis=1)

    def cross_rows(p):
        part = slice(PIECE * p, PIECE * p + PIECE)
        hot = jnp.where((row % 4).astype(F32) == task_row(p, owner_ref), 1.0, 0.0).T.astype(BF16)
        low = jnp.zeros((PIECE, 128), F32)
        for j in range(8):
            cols = slice(256 * j, 256 * j + 256)
            added = jnp.dot(hot, users[:, cols], preferred_element_type=F32)
            x0 = (x[part, cols].astype(F32) + added).astype(BF16)
            x[part, cols] = x0
            low = low + jnp.dot(x0, cross_u[cols, :], preferred_element_type=F32)
        left = jnp.concatenate([low.astype(BF16), ones], axis=1)
        if p == 0:
            get_v.wait()
        for j in range(8):
            cols = slice(256 * j, 256 * j + 256)
            cross = jnp.dot(left, cross_v[:, cols], preferred_element_type=F32)
            x[part, cols] = (x[part, cols].astype(F32) * cross).astype(BF16)

    quarter = lanes((1, 128)) // 32

    def expert_rows(p):
        part = slice(PIECE * p, PIECE * p + PIECE)
        task = task_row(p, task_ref)
        outs = []
        for k in range(EXPERTS):
            right = jnp.concatenate([w[0, k], w[1, k]], axis=1)
            active = jax.nn.relu(jnp.dot(x[part, :], right, preferred_element_type=F32)).astype(BF16)
            terms = lax.dot_general(heads, active, ROW_BY_ROW, preferred_element_type=F32)
            outs.append(jnp.sum(jnp.where(row.astype(F32) == task * EXPERTS + k, terms, 0.0), axis=0, keepdims=True))
        for half in range(2):
            stack = jnp.concatenate([o[:, 128 * half : 128 * half + 128] for o in outs] + [jnp.zeros((5, 128), F32)], axis=0)
            turns = [stack] + [pltpu.roll(stack, 32 * q, 1) for q in range(1, 4)]
            for q in range(4):
                message = jnp.zeros((1, 128), F32)
                for k in range(EXPERTS):
                    message = jnp.where(quarter == k, turns[(k - q) % 4][k : k + 1], message)
                out_ref[pl.ds(piece_chip(p, 4 * half + q), 1), :] = message

    arrivals[0].wait()
    get_u.wait()
    cross_rows(0)
    arrivals[1].wait()
    for copy in get_w:
        copy.wait()
    own = x[pl.ds(pl.multiple_of(lax.axis_index("z") * 32, 32), 32), :]
    logits = lax.dot_general(gate_ref[...], own, ROW_BY_ROW, preferred_element_type=F32)
    own_row = rows((16, 32))
    picked = jnp.where(own_row // EXPERTS == own_task_ref[...], jax.nn.sigmoid(logits), 0.0)
    gates = picked / jnp.sum(picked, axis=0, keepdims=True)
    row_of = jnp.zeros((1, 128), F32)
    for k in range(EXPERTS):
        gate = jnp.sum(jnp.where(own_row % EXPERTS == k, gates, 0.0), axis=0, keepdims=True)
        gate = widen(gate)
        row_of = row_of + (gate if k == 0 else turn(gate, 32 * k))
    gates_ref[...] = row_of
    cross_rows(1)
    expert_rows(0)
    for copy in arrivals[2:]:
        copy.wait()
    cross_rows(2)
    expert_rows(1)
    cross_rows(3)
    expert_rows(2)
    expert_rows(3)


def home_kernel(got_ref, gates_ref, owner_ref, out_ref):
    total = jnp.sum(got_ref[...], axis=0, keepdims=True) * gates_ref[...]
    total = total + turn(total, 64)
    total = total + turn(total, 32)
    out_ref[...] = jnp.where(owner_ref[...] < REQ_GRP, total[:, 0:32], 0.0)


def hold_kernel(x_ref, after_ref, out_ref):
    del x_ref, after_ref, out_ref


def hold(x, after):
    return pl.pallas_call(
        hold_kernel,
        out_shape=jax.ShapeDtypeStruct(x.shape, x.dtype),
        in_specs=[HBM, ANY],
        out_specs=HBM,
        input_output_aliases={0: 0},
        compiler_params=params(256),
    )(x, after)


def body(
    hist, tower_gain, up_w, down_w, query, proj_w, cand, owner, task, cross_u, cross_v, cross_bias, gate_w, expert_w, head_w,
):
    owner, task = owner[None, :], task[None, :]
    column = lax.all_gather(cand, "z", axis=0, tiled=True)
    message = pl.pallas_call(
        pack_kernel,
        out_shape=jax.ShapeDtypeStruct((160, 128), BF16),
        in_specs=[VMEM] * 4,
        out_specs=VMEM,
        compiler_params=params(64),
    )(hist.T, tower_gain, query[None, :], head_w.transpose(1, 0, 2))
    pair = lax.all_gather(message, "c", axis=0)
    spread, hist_c, query_c = pl.pallas_call(
        spread_kernel,
        out_shape=(
            jax.ShapeDtypeStruct((N_CHIPS, 72, 128), BF16),
            jax.ShapeDtypeStruct((64, 128), BF16),
            jax.ShapeDtypeStruct((8, 128), F32),
        ),
        in_specs=[VMEM] * 3,
        out_specs=(VMEM,) * 3,
        compiler_params=params(1024),
    )(pair, owner, task)
    tokens = lax.all_to_all(spread, CHIPS, 0, 0, tiled=True)
    swap = lambda x: lax.ppermute(x, "c", [(0, 1), (1, 0)])
    parts, owners, tasks = pl.pallas_call(
        tower_kernel,
        out_shape=(
            jax.ShapeDtypeStruct((N_CHIPS, 64, 128), BF16),
            jax.ShapeDtypeStruct((8, 128), F32),
            jax.ShapeDtypeStruct((8, 128), F32),
        ),
        in_specs=[VMEM] + [HBM] * 4,
        out_specs=(VMEM,) * 3,
        scratch_shapes=[
            pltpu.VMEM((2, 4096, 128), BF16),
            pltpu.VMEM((2, 128, 4096), BF16),
            pltpu.SemaphoreType.DMA((4,)),
        ],
        compiler_params=params(11264),
    )(tokens, up_w, swap(up_w), down_w, swap(down_w))
    summed = lax.all_to_all(parts, CHIPS, 0, 0, tiled=True)
    at = lambda x: (x % 2) * 2 + (x % 4) // 2
    shift = lambda x, by: lax.ppermute(x, ("xl", "xh"), [(at(i), at(i + by)) for i in range(4)])
    held = hold(column, owners)
    left, right = shift(held, 1), shift(held, 3)
    far0, far1 = shift(left[0:128], 1), shift(right[128:256], 3)
    values = pl.pallas_call(
        values_kernel,
        out_shape=jax.ShapeDtypeStruct((N_CHIPS, 40, 128), BF16),
        in_specs=[VMEM] * 3 + [HBM] * 2,
        out_specs=VMEM,
        scratch_shapes=[pltpu.VMEM((128, 2048), BF16), pltpu.SemaphoreType.DMA((2,))],
        compiler_params=params(1024),
    )(summed, hist_c, query_c, proj_w, swap(proj_w))
    values = lax.all_to_all(values, CHIPS, 0, 0, tiled=True)
    user = pl.pallas_call(
        user_kernel,
        out_shape=jax.ShapeDtypeStruct((64, 128), F32),
        in_specs=[VMEM],
        out_specs=VMEM,
        compiler_params=params(12288),
    )(values)
    users = lax.all_to_all(user, ALL, 0, 0, tiled=True)
    gate_rows = jnp.pad(gate_w.T, ((0, 4), (0, 0)))
    part, gates = pl.pallas_call(
        score_kernel,
        out_shape=(jax.ShapeDtypeStruct((N_CHIPS, 128), F32), jax.ShapeDtypeStruct((1, 128), F32)),
        in_specs=[VMEM] + [HBM] * 5 + [VMEM] * 4 + [HBM] * 2 + [VMEM] * 2 + [HBM] * 2,
        out_specs=(VMEM,) * 2,
        scratch_shapes=[
            pltpu.VMEM((16, 2048), BF16),
            pltpu.VMEM((4 * PIECE, 2048), BF16),
            pltpu.VMEM((2048, 128), BF16),
            pltpu.VMEM((256, 2048), BF16),
            pltpu.VMEM((2, EXPERTS, 2048, 128), BF16),
            pltpu.SemaphoreType.DMA((9,)),
        ],
        compiler_params=params(384),
    )(
        users, held, left, right, far0, far1, owners, tasks, task, pair, cross_u, cross_v, cross_bias[None, :],
        gate_rows, expert_w, swap(expert_w),
    )
    back = lax.all_to_all(part, CHIPS, 0, 0, tiled=True)
    score = pl.pallas_call(
        home_kernel,
        out_shape=jax.ShapeDtypeStruct((1, 32), F32),
        in_specs=[VMEM] * 3,
        out_specs=VMEM,
        compiler_params=params(256),
    )(back, gates, owner)
    return score[0]


def solution(mesh):
    fine = Mesh(mesh.devices.reshape(mesh.devices.shape[0], 8, 2, 2, 2), ("grp", "z", "xl", "xh", "c"))
    t = ("z", "xl", "xh", "c")
    in_specs = (
        P("grp", t),
        P(None, t),
        P(None, t),
        P(t, None),
        P(t),
        P(t, None),
        P(("grp",) + t, None),
        P(("grp",) + t),
        P(("grp",) + t),
        P(),
        P(),
        P(),
        P(),
        P(None, None, t),
        P(None, None, t),
    )
    return jax.shard_map(body, mesh=fine, in_specs=in_specs, out_specs=P(("grp",) + t), check_vma=False)
```

```python
import math

import jax
import jax.numpy as jnp
from jax import lax
from jax.experimental import pallas as pl
from jax.experimental.pallas import tpu as pltpu
from jax.sharding import Mesh, PartitionSpec as P

D = 4096
EXPERTS = 3
TASKS = 4
REQ_GRP = 4
HIST = 32
epsilon = 1e-05

CHIPS = ("z", "xh", "xl")
ALL = ("z", "xh", "xl", "c")
N_CHIPS = 32
F32 = jnp.float32
BF16 = jnp.bfloat16
HIGH = lax.Precision.HIGHEST

VMEM = pl.BlockSpec(memory_space=pltpu.VMEM)
ANY = pl.BlockSpec(memory_space=pl.ANY)
HBM = pl.BlockSpec(memory_space=pltpu.HBM)
ROW_BY_ROW = (((1,), (1,)), ((), ()))


def params(room_kib):
    return pltpu.CompilerParams(vmem_limit_bytes=(64 << 20) - (room_kib << 10))


def block_of(chip):
    return (chip & ~3) | ((chip & 1) << 1) | ((chip >> 1) & 1)


def split2(x):
    high = x.astype(BF16).astype(F32)
    return high, x - high


def lanes(shape):
    return lax.broadcasted_iota(jnp.int32, shape, len(shape) - 1)


def rows(shape):
    return lax.broadcasted_iota(jnp.int32, shape, len(shape) - 2)


def token_sums(x):
    padded = jnp.concatenate([x, jnp.zeros((128 - x.shape[0], 128), F32)], axis=0)
    return lax.dot_general(jnp.ones((8, 128), F32), padded, ROW_BY_ROW, precision=HIGH, preferred_element_type=F32)


def turn(x, by):
    return pltpu.roll(jnp.broadcast_to(x, (8, 128)), by, 1)[0:1]


def widen(x):
    return jnp.concatenate([x, jnp.zeros((1, 128 - x.shape[1]), x.dtype)], axis=1)


def pack_kernel(hist_ref, gain_ref, query_ref, head_ref, out_ref):
    hist = hist_ref[...].astype(F32)
    out_ref[0:128, :] = jnp.concatenate([hist, jnp.zeros((64, 128), F32)], axis=0).T.astype(BF16)
    row = rows((16, 128))
    ends = jnp.concatenate([gain_ref[...].astype(F32), query_ref[...].astype(F32)], axis=1)
    out_ref[128:144, :] = jnp.where(row == 0, ends, 0.0).astype(BF16)
    heads = jnp.zeros((16, 128), F32)
    for k in range(EXPERTS):
        head = head_ref[k].astype(F32)
        for t in range(TASKS):
            heads = jnp.where(row == t * EXPERTS + k, head[t : t + 1], heads)
    out_ref[144:160, :] = heads.astype(BF16)


def spread_kernel(pair_ref, out_ref, hist_ref, query_ref):
    core = lax.axis_index("c")
    tokens = pl.ds(pl.multiple_of(core * 64, 64), 64)
    first = pair_ref[0, tokens, :].astype(F32)
    second = pair_ref[1, tokens, :].astype(F32)
    hist = jnp.where(lanes((64, 128)) < 64, first, pltpu.roll(second, 64, 1))
    head0 = pair_ref[0, 128:144, :].astype(F32)[0:1]
    head1 = pair_ref[1, 128:144, :].astype(F32)[0:1]
    low = lanes((1, 128)) < 64
    gain = jnp.where(low, head0, turn(head1, 64))
    query = jnp.where(low, turn(head0, 64), head1)
    scaled = (hist * gain).astype(BF16)
    high, rest = split2(token_sums(hist * hist))
    row = rows((8, 128))
    extra = jnp.where(row == 0, high, jnp.where(row == 1, rest, 0.0)).astype(BF16)
    for chip in range(N_CHIPS):
        out_ref[chip, 0:64, :] = scaled
        out_ref[chip, 64:72, :] = extra
    hist_ref[...] = hist.astype(BF16)
    query_ref[...] = jnp.broadcast_to(query, (8, 128))


def tower_kernel(got_ref, up0_ref, up1_ref, down0_ref, down1_ref, out_ref, down, sems):
    copies = []
    for i, source in enumerate((down0_ref, down1_ref)):
        copies.append(pltpu.make_async_copy(source, down.at[128 * i : 128 * i + 128, :], sems.at[i]))
    for copy in copies:
        copy.start()
    stats = jnp.zeros((8, 128), F32)
    for chip in range(N_CHIPS):
        stats = stats + got_ref[chip, 64:72, :].astype(F32)
    inverse = lax.rsqrt((stats[0:1] + stats[1:2]) / D + epsilon)
    column = jnp.broadcast_to(inverse, (128, 128)).T[0:64]
    total = jnp.zeros((64, 256), F32)
    for b in range(0, N_CHIPS, 2):
        left = jnp.concatenate([got_ref[block_of(b), 0:64, :], got_ref[block_of(b + 1), 0:64, :]], axis=1)
        part = slice(b * 128, b * 128 + 256)
        right = jnp.concatenate([up0_ref[part, :], up1_ref[part, :]], axis=1)
        total = total + jnp.dot(left, right, preferred_element_type=F32)
    hidden = jax.nn.gelu(total * jnp.concatenate([column, column], axis=1)).astype(BF16)
    for copy in copies:
        copy.wait()
    for b in range(0, N_CHIPS, 2):
        part = jnp.dot(hidden, down[:, b * 128 : b * 128 + 256], preferred_element_type=F32).astype(BF16)
        out_ref[block_of(b), :, :] = part[:, 0:128]
        out_ref[block_of(b + 1), :, :] = part[:, 128:256]


def values_kernel(got_ref, hist_ref, query_ref, proj0_ref, proj1_ref, out_ref, proj, sems):
    copies = []
    for i, source in enumerate((proj0_ref, proj1_ref)):
        copies.append(pltpu.make_async_copy(source, proj.at[64 * i : 64 * i + 64, :], sems.at[i]))
    for copy in copies:
        copy.start()
    core = lax.axis_index("c")
    summed = got_ref[0].astype(F32)
    for chip in range(1, N_CHIPS):
        summed = summed + got_ref[chip].astype(F32)
    tower = (hist_ref[...].astype(F32) + summed).astype(BF16).astype(F32)
    square_high, square_rest = split2(token_sums(tower * tower))
    dot_high, dot_rest = split2(token_sums(tower * query_ref[0:1, :]))
    row = rows((8, 128))
    extra = jnp.where(row == 2, dot_high, jnp.where(row == 3, dot_rest, 0.0))
    extra = jnp.where(row == 0, square_high, jnp.where(row == 1, square_rest, extra)).astype(BF16)
    mine = jnp.where(core == 0, tower, pltpu.roll(tower, 64, 1)).astype(BF16)
    low = lanes((32, 128)) < 64
    for copy in copies:
        copy.wait()
    for j in range(16):
        part = jnp.dot(mine, proj[:, 128 * j : 128 * j + 128], preferred_element_type=F32)
        turned = pltpu.roll(part, 64, 1)
        out_ref[2 * j, 0:32, :] = jnp.where(low, part[0:32], turned[32:64]).astype(BF16)
        out_ref[2 * j + 1, 0:32, :] = jnp.where(low, turned[0:32], part[32:64]).astype(BF16)
        out_ref[2 * j, 32:40, :] = extra
        out_ref[2 * j + 1, 32:40, :] = extra


def user_kernel(got_ref, owner_ref, task_ref, out_ref):
    values = got_ref[0, 0:32, :].astype(F32)
    stats = got_ref[0, 32:40, :].astype(F32)
    for chip in range(1, N_CHIPS):
        values = values + got_ref[chip, 0:32, :].astype(F32)
        stats = stats + got_ref[chip, 32:40, :].astype(F32)
    squares = stats[0:1] + stats[1:2]
    dotted = stats[2:3] + stats[3:4]
    weight = jax.nn.sigmoid(dotted * lax.rsqrt(squares / D + epsilon))
    column = jnp.broadcast_to(weight, (128, 128)).T
    weights = jnp.where(lanes((32, 128)) < 64, column[0:32], column[32:64])
    user = jnp.sum(weights * values, axis=0, keepdims=True) / math.sqrt(HIST)
    slots = widen(owner_ref[...].astype(F32)) + turn(widen(task_ref[...].astype(F32)), 32)
    slots = slots + turn(slots, 64)
    out_ref[...] = jnp.where(rows((128, 128)) % 2 == 0, user, slots)


SLOTS = 1024
HALF = 512


def score_kernel(
    got_ref, cand_ref, own_task_ref, pair_ref, cross_u_ref, cross_v_ref, bias_ref, gate_ref, w0_ref, w1_ref,
    out_ref, gates_ref, users, x, cross_u, cross_v, w, sems,
):
    core = lax.axis_index("c")
    chip_here = lax.axis_index("z") * 4 + lax.axis_index("xh") * 2 + lax.axis_index("xl")

    def piece(i):
        part = slice(HALF * i, HALF * i + HALF)
        return pltpu.make_async_copy(cand_ref.at[part, :], x.at[part, :], sems.at[i])

    arrivals = [piece(0), piece(1)]
    get_u = pltpu.make_async_copy(cross_u_ref, cross_u, sems.at[2])
    get_v = pltpu.make_async_copy(cross_v_ref, cross_v.at[0:128, :], sems.at[3])
    get_w = []
    for k in range(EXPERTS):
        for i, source in enumerate((w0_ref, w1_ref)):
            start = 256 * k + 128 * i
            get_w.append(pltpu.make_async_copy(source.at[k], w.at[:, start : start + 128], sems.at[4 + 2 * k + i]))
    for copy in (arrivals[0], get_u, get_v, arrivals[1], *get_w):
        copy.start()
    row = rows((16, 128))
    low_half = lanes((1, 128)) < 64
    for j in range(16):
        full = jnp.zeros((16, 128), F32)
        for c in range(2):
            first = got_ref[8 * j + 2 * c : 8 * j + 2 * c + 1, :]
            second = got_ref[8 * j + 4 + 2 * c : 8 * j + 5 + 2 * c, :]
            full = jnp.where(row % 4 == 2 * c, jnp.where(low_half, first, turn(second, 64)), full)
            full = jnp.where(row % 4 == 2 * c + 1, jnp.where(low_half, turn(first, 64), second), full)
        high, rest = split2(full)
        mid, last = split2(rest)
        users[:, 128 * j : 128 * j + 128] = jnp.where(
            row < 4, high, jnp.where(row < 8, mid, jnp.where(row < 12, last, 0.0))
        ).astype(BF16)
    quarter = lanes((1, 128)) // 32
    owners, tasks = [], []
    for b in range(8):
        owner = jnp.zeros((1, 128), F32)
        task = jnp.zeros((1, 128), F32)
        for q in range(4):
            slots = got_ref[pl.ds(4 * (4 * b + q) + 2 * core + 1, 1), :]
            turned = turn(slots, 32)
            owner = jnp.where(quarter == q, (slots, turned)[q % 2], owner)
            task = jnp.where(quarter == q, (turned, slots)[q % 2], task)
        owners.append(owner)
        tasks.append(task)
    owners = jnp.concatenate(owners, axis=1)
    tasks = jnp.concatenate(tasks, axis=1)
    heads = jnp.concatenate([pair_ref[core, 144:160, :], pair_ref[1 - core, 144:160, :]], axis=1)
    row = rows((16, 2048))
    bias = bias_ref[...].astype(F32)
    cross_v[128:144, :] = jnp.where(row == 0, bias, jnp.where(row == 1, 1.0, 0.0)).astype(BF16)
    cross_v[144:256, :] = jnp.zeros((112, 2048), BF16)
    ones = jnp.where(lanes((HALF, 128)) < 2, 1.0, 0.0).astype(BF16)
    row = rows((16, HALF))
    for i in range(2):
        part = slice(HALF * i, HALF * i + HALF)
        hot = jnp.where((row % 4).astype(F32) == owners[:, part], 1.0, 0.0).T.astype(BF16)
        arrivals[i].wait()
        for j in range(4):
            cols = slice(512 * j, 512 * j + 512)
            added = jnp.dot(hot, users[:, cols], preferred_element_type=F32)
            x[part, cols] = (x[part, cols].astype(F32) + added).astype(BF16)
        if i == 0:
            get_u.wait()
        low = jnp.dot(x[part, :], cross_u[...], preferred_element_type=F32).astype(BF16)
        left = jnp.concatenate([low, ones], axis=1)
        if i == 0:
            get_v.wait()
        for j in range(4):
            cols = slice(512 * j, 512 * j + 512)
            cross = jnp.dot(left, cross_v[:, cols], preferred_element_type=F32)
            x[part, cols] = (x[part, cols].astype(F32) * cross).astype(BF16)
    own = x[pl.ds(pl.multiple_of(chip_here * 32, 32), 32), :]
    logits = lax.dot_general(gate_ref[...], own, ROW_BY_ROW, preferred_element_type=F32)
    row = rows((16, 32))
    picked = jnp.where(row // EXPERTS == own_task_ref[...], jax.nn.sigmoid(logits), 0.0)
    gates = picked / jnp.sum(picked, axis=0, keepdims=True)
    row_of = jnp.zeros((1, 128), F32)
    for k in range(EXPERTS):
        gate = widen(jnp.sum(jnp.where(row % EXPERTS == k, gates, 0.0), axis=0, keepdims=True))
        row_of = row_of + (gate if k == 0 else turn(gate, 32 * k))
    gates_ref[...] = row_of
    for copy in get_w:
        copy.wait()
    active = jax.nn.relu(jnp.dot(x[...], w[...], preferred_element_type=F32)).astype(BF16)
    row = rows((16, SLOTS)).astype(F32)
    outs = []
    for k in range(EXPERTS):
        terms = lax.dot_general(heads, active[:, 256 * k : 256 * k + 256], ROW_BY_ROW, preferred_element_type=F32)
        outs.append(jnp.sum(jnp.where(row == tasks * EXPERTS + k, terms, 0.0), axis=0, keepdims=True))
    for b in range(8):
        stack = jnp.concatenate([o[:, 128 * b : 128 * b + 128] for o in outs] + [jnp.zeros((5, 128), F32)], axis=0)
        turns = [stack] + [pltpu.roll(stack, 32 * q, 1) for q in range(1, 4)]
        for q in range(4):
            message = jnp.zeros((1, 128), F32)
            for k in range(EXPERTS):
                message = jnp.where(quarter == k, turns[(k - q) % 4][k : k + 1], message)
            out_ref[4 * b + q : 4 * b + q + 1, :] = message


def home_kernel(got_ref, gates_ref, owner_ref, out_ref):
    total = jnp.sum(got_ref[...], axis=0, keepdims=True) * gates_ref[...]
    total = total + turn(total, 64)
    total = total + turn(total, 32)
    out_ref[...] = jnp.where(owner_ref[...] < REQ_GRP, total[:, 0:32], 0.0)


def body(
    hist, tower_gain, up_w, down_w, query, proj_w, cand, owner, task, cross_u, cross_v, cross_bias, gate_w, expert_w, head_w,
):
    owner, task = owner[None, :], task[None, :]
    everyone = lax.all_gather(cand, CHIPS, axis=0, tiled=True)
    message = pl.pallas_call(
        pack_kernel,
        out_shape=jax.ShapeDtypeStruct((160, 128), BF16),
        in_specs=[VMEM] * 4,
        out_specs=VMEM,
        compiler_params=params(64),
    )(hist.T, tower_gain, query[None, :], head_w.transpose(1, 0, 2))
    pair = lax.all_gather(message, "c", axis=0)
    spread, hist_c, query_c = pl.pallas_call(
        spread_kernel,
        out_shape=(
            jax.ShapeDtypeStruct((N_CHIPS, 72, 128), BF16),
            jax.ShapeDtypeStruct((64, 128), BF16),
            jax.ShapeDtypeStruct((8, 128), F32),
        ),
        in_specs=[VMEM],
        out_specs=(VMEM,) * 3,
        compiler_params=params(63 << 10),
    )(pair)
    tokens = lax.all_to_all(spread, CHIPS, 0, 0, tiled=True)
    swap = lambda x: lax.ppermute(x, "c", [(0, 1), (1, 0)])
    parts = pl.pallas_call(
        tower_kernel,
        out_shape=jax.ShapeDtypeStruct((N_CHIPS, 64, 128), BF16),
        in_specs=[VMEM] * 3 + [HBM] * 2,
        out_specs=VMEM,
        scratch_shapes=[pltpu.VMEM((256, 4096), BF16), pltpu.SemaphoreType.DMA((2,))],
        compiler_params=params(13900),
    )(tokens, up_w, swap(up_w), down_w, swap(down_w))
    summed = lax.all_to_all(parts, CHIPS, 0, 0, tiled=True)
    values = pl.pallas_call(
        values_kernel,
        out_shape=jax.ShapeDtypeStruct((N_CHIPS, 40, 128), BF16),
        in_specs=[VMEM] * 3 + [HBM] * 2,
        out_specs=VMEM,
        scratch_shapes=[pltpu.VMEM((128, 2048), BF16), pltpu.SemaphoreType.DMA((2,))],
        compiler_params=params(12160),
    )(summed, hist_c, query_c, proj_w, swap(proj_w))
    values = lax.all_to_all(values, CHIPS, 0, 0, tiled=True)
    user = pl.pallas_call(
        user_kernel,
        out_shape=jax.ShapeDtypeStruct((128, 128), F32),
        in_specs=[VMEM] * 3,
        out_specs=VMEM,
        compiler_params=params(12288),
    )(values, owner, task)
    users = lax.all_to_all(user, ALL, 0, 0, tiled=True)
    gate_rows = jnp.pad(gate_w.T, ((0, 4), (0, 0)))
    part, gates = pl.pallas_call(
        score_kernel,
        out_shape=(jax.ShapeDtypeStruct((N_CHIPS, 128), F32), jax.ShapeDtypeStruct((1, 128), F32)),
        in_specs=[VMEM, HBM, VMEM, VMEM, HBM, HBM, VMEM, VMEM, HBM, HBM],
        out_specs=(VMEM,) * 2,
        scratch_shapes=[
            pltpu.VMEM((16, 2048), BF16),
            pltpu.VMEM((SLOTS, 2048), BF16),
            pltpu.VMEM((2048, 128), BF16),
            pltpu.VMEM((256, 2048), BF16),
            pltpu.VMEM((2048, 768), BF16),
            pltpu.SemaphoreType.DMA((10,)),
        ],
        compiler_params=params(11700),
    )(users, everyone, task, pair, cross_u, cross_v, cross_bias[None, :], gate_rows, expert_w, swap(expert_w))
    back = lax.all_to_all(part, CHIPS, 0, 0, tiled=True)
    score = pl.pallas_call(
        home_kernel,
        out_shape=jax.ShapeDtypeStruct((1, 32), F32),
        in_specs=[VMEM] * 3,
        out_specs=VMEM,
        compiler_params=params(12288),
    )(back, gates, owner)
    return score[0]


def solution(mesh):
    fine = Mesh(mesh.devices.reshape(mesh.devices.shape[0], 8, 2, 2, 2), ("grp", "z", "xl", "xh", "c"))
    t = ("z", "xl", "xh", "c")
    in_specs = (
        P("grp", t),
        P(None, t),
        P(None, t),
        P(t, None),
        P(t),
        P(t, None),
        P(("grp",) + t, None),
        P(("grp",) + t),
        P(("grp",) + t),
        P(),
        P(),
        P(),
        P(),
        P(None, None, t),
        P(None, None, t),
    )
    return jax.shard_map(body, mesh=fine, in_specs=in_specs, out_specs=P(("grp",) + t), check_vma=False)
```

```python
import math

import jax
import jax.numpy as jnp
from jax import lax
from jax.experimental import pallas as pl
from jax.experimental.pallas import tpu as pltpu
from jax.sharding import Mesh, PartitionSpec as P

D = 4096
EXPERTS = 3
TASKS = 4
REQ_GRP = 4
HIST = 32
epsilon = 1e-05

CHIPS = ("z", "xh", "xl")
ALL = ("z", "xh", "xl", "c")
N_CHIPS = 32
F32 = jnp.float32
BF16 = jnp.bfloat16
HIGH = lax.Precision.HIGHEST

VMEM = pl.BlockSpec(memory_space=pltpu.VMEM)
ANY = pl.BlockSpec(memory_space=pl.ANY)
HBM = pl.BlockSpec(memory_space=pltpu.HBM)
ROW_BY_ROW = (((1,), (1,)), ((), ()))


def params(room_kib):
    return pltpu.CompilerParams(vmem_limit_bytes=(64 << 20) - (room_kib << 10))


def block_of(chip):
    return (chip & ~3) | ((chip & 1) << 1) | ((chip >> 1) & 1)


def split2(x):
    high = x.astype(BF16).astype(F32)
    return high, x - high


def lanes(shape):
    return lax.broadcasted_iota(jnp.int32, shape, len(shape) - 1)


def rows(shape):
    return lax.broadcasted_iota(jnp.int32, shape, len(shape) - 2)


def token_sums(x):
    padded = jnp.concatenate([x, jnp.zeros((128 - x.shape[0], 128), F32)], axis=0)
    return lax.dot_general(jnp.ones((8, 128), F32), padded, ROW_BY_ROW, precision=HIGH, preferred_element_type=F32)


def turn(x, by):
    return pltpu.roll(jnp.broadcast_to(x, (8, 128)), by, 1)[0:1]


def widen(x):
    return jnp.concatenate([x, jnp.zeros((1, 128 - x.shape[1]), x.dtype)], axis=1)


def pack_kernel(hist_ref, gain_ref, query_ref, head_ref, out_ref):
    hist = hist_ref[...].astype(F32)
    out_ref[0:128, :] = jnp.concatenate([hist, jnp.zeros((64, 128), F32)], axis=0).T.astype(BF16)
    row = rows((16, 128))
    ends = jnp.concatenate([gain_ref[...].astype(F32), query_ref[...].astype(F32)], axis=1)
    out_ref[128:144, :] = jnp.where(row == 0, ends, 0.0).astype(BF16)
    heads = jnp.zeros((16, 128), F32)
    for k in range(EXPERTS):
        head = head_ref[k].astype(F32)
        for t in range(TASKS):
            heads = jnp.where(row == t * EXPERTS + k, head[t : t + 1], heads)
    out_ref[144:160, :] = heads.astype(BF16)


def spread_kernel(pair_ref, out_ref, hist_ref, query_ref):
    core = lax.axis_index("c")
    tokens = pl.ds(pl.multiple_of(core * 64, 64), 64)
    first = pair_ref[0, tokens, :].astype(F32)
    second = pair_ref[1, tokens, :].astype(F32)
    hist = jnp.where(lanes((64, 128)) < 64, first, pltpu.roll(second, 64, 1))
    head0 = pair_ref[0, 128:144, :].astype(F32)[0:1]
    head1 = pair_ref[1, 128:144, :].astype(F32)[0:1]
    low = lanes((1, 128)) < 64
    gain = jnp.where(low, head0, turn(head1, 64))
    query = jnp.where(low, turn(head0, 64), head1)
    scaled = (hist * gain).astype(BF16)
    high, rest = split2(token_sums(hist * hist))
    row = rows((8, 128))
    extra = jnp.where(row == 0, high, jnp.where(row == 1, rest, 0.0)).astype(BF16)
    for chip in range(N_CHIPS):
        out_ref[chip, 0:64, :] = scaled
        out_ref[chip, 64:72, :] = extra
    hist_ref[...] = hist.astype(BF16)
    query_ref[...] = jnp.broadcast_to(query, (8, 128))


def tower_kernel(got_ref, up0_ref, up1_ref, down0_ref, down1_ref, out_ref, down, sems):
    copies = []
    for i, source in enumerate((down0_ref, down1_ref)):
        copies.append(pltpu.make_async_copy(source, down.at[128 * i : 128 * i + 128, :], sems.at[i]))
    for copy in copies:
        copy.start()
    stats = jnp.zeros((8, 128), F32)
    for chip in range(N_CHIPS):
        stats = stats + got_ref[chip, 64:72, :].astype(F32)
    inverse = lax.rsqrt((stats[0:1] + stats[1:2]) / D + epsilon)
    column = jnp.broadcast_to(inverse, (128, 128)).T[0:64]
    left = jnp.concatenate([got_ref[block_of(b), 0:64, :] for b in range(N_CHIPS)], axis=1)
    total = jnp.concatenate(
        [jnp.dot(left, up[...], preferred_element_type=F32) for up in (up0_ref, up1_ref)], axis=1
    )
    hidden = jax.nn.gelu(total * jnp.concatenate([column, column], axis=1)).astype(BF16)
    for copy in copies:
        copy.wait()
    part = jnp.dot(hidden, down[...], preferred_element_type=F32).astype(BF16)
    for b in range(N_CHIPS):
        out_ref[block_of(b), :, :] = part[:, 128 * b : 128 * b + 128]


def values_kernel(got_ref, hist_ref, query_ref, proj0_ref, proj1_ref, out_ref, proj, sems):
    copies = []
    for i, source in enumerate((proj0_ref, proj1_ref)):
        copies.append(pltpu.make_async_copy(source, proj.at[64 * i : 64 * i + 64, :], sems.at[i]))
    for copy in copies:
        copy.start()
    core = lax.axis_index("c")
    summed = got_ref[0].astype(F32)
    for chip in range(1, N_CHIPS):
        summed = summed + got_ref[chip].astype(F32)
    tower = (hist_ref[...].astype(F32) + summed).astype(BF16).astype(F32)
    square_high, square_rest = split2(token_sums(tower * tower))
    dot_high, dot_rest = split2(token_sums(tower * query_ref[0:1, :]))
    row = rows((8, 128))
    extra = jnp.where(row == 2, dot_high, jnp.where(row == 3, dot_rest, 0.0))
    extra = jnp.where(row == 0, square_high, jnp.where(row == 1, square_rest, extra)).astype(BF16)
    mine = jnp.where(core == 0, tower, pltpu.roll(tower, 64, 1)).astype(BF16)
    low = lanes((32, 128)) < 64
    for copy in copies:
        copy.wait()
    for j in range(16):
        part = jnp.dot(mine, proj[:, 128 * j : 128 * j + 128], preferred_element_type=F32)
        turned = pltpu.roll(part, 64, 1)
        out_ref[2 * j, 0:32, :] = jnp.where(low, part[0:32], turned[32:64]).astype(BF16)
        out_ref[2 * j + 1, 0:32, :] = jnp.where(low, turned[0:32], part[32:64]).astype(BF16)
        out_ref[2 * j, 32:40, :] = extra
        out_ref[2 * j + 1, 32:40, :] = extra


def user_kernel(got_ref, owner_ref, task_ref, out_ref):
    values = got_ref[0, 0:32, :].astype(F32)
    stats = got_ref[0, 32:40, :].astype(F32)
    for chip in range(1, N_CHIPS):
        values = values + got_ref[chip, 0:32, :].astype(F32)
        stats = stats + got_ref[chip, 32:40, :].astype(F32)
    squares = stats[0:1] + stats[1:2]
    dotted = stats[2:3] + stats[3:4]
    weight = jax.nn.sigmoid(dotted * lax.rsqrt(squares / D + epsilon))
    column = jnp.broadcast_to(weight, (128, 128)).T
    weights = jnp.where(lanes((32, 128)) < 64, column[0:32], column[32:64])
    user = jnp.sum(weights * values, axis=0, keepdims=True) / math.sqrt(HIST)
    slots = widen(owner_ref[...].astype(F32)) + turn(widen(task_ref[...].astype(F32)), 32)
    slots = slots + turn(slots, 64)
    out_ref[...] = jnp.where(rows((128, 128)) % 2 == 0, user, slots)


SLOTS = 1024
STEP = 256


def score_kernel(
    got_ref, cand_ref, own_task_ref, pair_ref, cross_u_ref, cross_v_ref, bias_ref, gate_ref, w0_ref, w1_ref,
    out_ref, gates_ref, users, x, cross_u, cross_v, w, sems,
):
    core = lax.axis_index("c")
    chip_here = lax.axis_index("z") * 4 + lax.axis_index("xh") * 2 + lax.axis_index("xl")

    def piece(i):
        part = slice(STEP * i, STEP * i + STEP)
        return pltpu.make_async_copy(cand_ref.at[part, :], x.at[part, :], sems.at[i])

    arrivals = [piece(i) for i in range(4)]
    get_u = pltpu.make_async_copy(cross_u_ref, cross_u, sems.at[4])
    get_v = pltpu.make_async_copy(cross_v_ref, cross_v.at[0:128, :], sems.at[5])
    get_w = []
    for k in range(EXPERTS):
        for i, source in enumerate((w0_ref, w1_ref)):
            start = 256 * k + 128 * i
            get_w.append(pltpu.make_async_copy(source.at[k], w.at[:, start : start + 128], sems.at[6 + 2 * k + i]))
    for copy in (arrivals[0], get_u, get_v, *arrivals[1:], *get_w):
        copy.start()
    row = rows((16, 128))
    low_half = lanes((1, 128)) < 64
    for j in range(16):
        full = jnp.zeros((16, 128), F32)
        for c in range(2):
            first = got_ref[8 * j + 2 * c : 8 * j + 2 * c + 1, :]
            second = got_ref[8 * j + 4 + 2 * c : 8 * j + 5 + 2 * c, :]
            full = jnp.where(row % 4 == 2 * c, jnp.where(low_half, first, turn(second, 64)), full)
            full = jnp.where(row % 4 == 2 * c + 1, jnp.where(low_half, turn(first, 64), second), full)
        high, rest = split2(full)
        mid, last = split2(rest)
        users[:, 128 * j : 128 * j + 128] = jnp.where(
            row < 4, high, jnp.where(row < 8, mid, jnp.where(row < 12, last, 0.0))
        ).astype(BF16)
    quarter = lanes((1, 128)) // 32
    owners, tasks = [], []
    for b in range(8):
        owner = jnp.zeros((1, 128), F32)
        task = jnp.zeros((1, 128), F32)
        for q in range(4):
            slots = got_ref[pl.ds(4 * (4 * b + q) + 2 * core + 1, 1), :]
            turned = turn(slots, 32)
            owner = jnp.where(quarter == q, (slots, turned)[q % 2], owner)
            task = jnp.where(quarter == q, (turned, slots)[q % 2], task)
        owners.append(owner)
        tasks.append(task)
    owners = jnp.concatenate(owners, axis=1)
    tasks = jnp.concatenate(tasks, axis=1)
    heads = jnp.concatenate([pair_ref[core, 144:160, :], pair_ref[1 - core, 144:160, :]], axis=1)
    row = rows((16, 2048))
    bias = bias_ref[...].astype(F32)
    cross_v[128:144, :] = jnp.where(row == 0, bias, jnp.where(row == 1, 1.0, 0.0)).astype(BF16)
    cross_v[144:256, :] = jnp.zeros((112, 2048), BF16)
    ones = jnp.where(lanes((STEP, 128)) < 2, 1.0, 0.0).astype(BF16)
    row = rows((16, STEP))
    for i in range(4):
        part = slice(STEP * i, STEP * i + STEP)
        hot = jnp.where((row % 4).astype(F32) == owners[:, part], 1.0, 0.0).T.astype(BF16)
        arrivals[i].wait()
        if i == 0:
            get_u.wait()
        low = jnp.zeros((STEP, 128), F32)
        for j in range(8):
            cols = slice(256 * j, 256 * j + 256)
            added = jnp.dot(hot, users[:, cols], preferred_element_type=F32)
            x0 = (x[part, cols].astype(F32) + added).astype(BF16)
            x[part, cols] = x0
            low = low + jnp.dot(x0, cross_u[cols, :], preferred_element_type=F32)
        left = jnp.concatenate([low.astype(BF16), ones], axis=1)
        if i == 0:
            get_v.wait()
        for j in range(8):
            cols = slice(256 * j, 256 * j + 256)
            cross = jnp.dot(left, cross_v[:, cols], preferred_element_type=F32)
            x[part, cols] = (x[part, cols].astype(F32) * cross).astype(BF16)
    own = x[pl.ds(pl.multiple_of(chip_here * 32, 32), 32), :]
    logits = lax.dot_general(gate_ref[...], own, ROW_BY_ROW, preferred_element_type=F32)
    row = rows((16, 32))
    picked = jnp.where(row // EXPERTS == own_task_ref[...], jax.nn.sigmoid(logits), 0.0)
    gates = picked / jnp.sum(picked, axis=0, keepdims=True)
    row_of = jnp.zeros((1, 128), F32)
    for k in range(EXPERTS):
        gate = widen(jnp.sum(jnp.where(row % EXPERTS == k, gates, 0.0), axis=0, keepdims=True))
        row_of = row_of + (gate if k == 0 else turn(gate, 32 * k))
    gates_ref[...] = row_of
    for copy in get_w:
        copy.wait()
    active = jax.nn.relu(jnp.dot(x[...], w[...], preferred_element_type=F32)).astype(BF16)
    row = rows((16, SLOTS)).astype(F32)
    outs = []
    for k in range(EXPERTS):
        terms = lax.dot_general(heads, active[:, 256 * k : 256 * k + 256], ROW_BY_ROW, preferred_element_type=F32)
        outs.append(jnp.sum(jnp.where(row == tasks * EXPERTS + k, terms, 0.0), axis=0, keepdims=True))
    for b in range(8):
        stack = jnp.concatenate([o[:, 128 * b : 128 * b + 128] for o in outs] + [jnp.zeros((5, 128), F32)], axis=0)
        turns = [stack] + [pltpu.roll(stack, 32 * q, 1) for q in range(1, 4)]
        for q in range(4):
            message = jnp.zeros((1, 128), F32)
            for k in range(EXPERTS):
                message = jnp.where(quarter == k, turns[(k - q) % 4][k : k + 1], message)
            out_ref[4 * b + q : 4 * b + q + 1, :] = message


def home_kernel(got_ref, gates_ref, owner_ref, out_ref):
    total = jnp.sum(got_ref[...], axis=0, keepdims=True) * gates_ref[...]
    total = total + turn(total, 64)
    total = total + turn(total, 32)
    out_ref[...] = jnp.where(owner_ref[...] < REQ_GRP, total[:, 0:32], 0.0)


def body(
    hist, tower_gain, up_w, down_w, query, proj_w, cand, owner, task, cross_u, cross_v, cross_bias, gate_w, expert_w, head_w,
):
    owner, task = owner[None, :], task[None, :]
    everyone = lax.all_gather(cand, CHIPS, axis=0, tiled=True)
    message = pl.pallas_call(
        pack_kernel,
        out_shape=jax.ShapeDtypeStruct((160, 128), BF16),
        in_specs=[VMEM] * 4,
        out_specs=VMEM,
        compiler_params=params(64),
    )(hist.T, tower_gain, query[None, :], head_w.transpose(1, 0, 2))
    pair = lax.all_gather(message, "c", axis=0)
    spread, hist_c, query_c = pl.pallas_call(
        spread_kernel,
        out_shape=(
            jax.ShapeDtypeStruct((N_CHIPS, 72, 128), BF16),
            jax.ShapeDtypeStruct((64, 128), BF16),
            jax.ShapeDtypeStruct((8, 128), F32),
        ),
        in_specs=[VMEM],
        out_specs=(VMEM,) * 3,
        compiler_params=params(63 << 10),
    )(pair)
    tokens = lax.all_to_all(spread, CHIPS, 0, 0, tiled=True)
    swap = lambda x: lax.ppermute(x, "c", [(0, 1), (1, 0)])
    parts = pl.pallas_call(
        tower_kernel,
        out_shape=jax.ShapeDtypeStruct((N_CHIPS, 64, 128), BF16),
        in_specs=[VMEM] * 3 + [HBM] * 2,
        out_specs=VMEM,
        scratch_shapes=[pltpu.VMEM((256, 4096), BF16), pltpu.SemaphoreType.DMA((2,))],
        compiler_params=params(13900),
    )(tokens, up_w, swap(up_w), down_w, swap(down_w))
    summed = lax.all_to_all(parts, CHIPS, 0, 0, tiled=True)
    values = pl.pallas_call(
        values_kernel,
        out_shape=jax.ShapeDtypeStruct((N_CHIPS, 40, 128), BF16),
        in_specs=[VMEM] * 3 + [HBM] * 2,
        out_specs=VMEM,
        scratch_shapes=[pltpu.VMEM((128, 2048), BF16), pltpu.SemaphoreType.DMA((2,))],
        compiler_params=params(12160),
    )(summed, hist_c, query_c, proj_w, swap(proj_w))
    values = lax.all_to_all(values, CHIPS, 0, 0, tiled=True)
    user = pl.pallas_call(
        user_kernel,
        out_shape=jax.ShapeDtypeStruct((128, 128), F32),
        in_specs=[VMEM] * 3,
        out_specs=VMEM,
        compiler_params=params(12288),
    )(values, owner, task)
    users = lax.all_to_all(user, ALL, 0, 0, tiled=True)
    gate_rows = jnp.pad(gate_w.T, ((0, 4), (0, 0)))
    part, gates = pl.pallas_call(
        score_kernel,
        out_shape=(jax.ShapeDtypeStruct((N_CHIPS, 128), F32), jax.ShapeDtypeStruct((1, 128), F32)),
        in_specs=[VMEM, HBM, VMEM, VMEM, HBM, HBM, VMEM, VMEM, HBM, HBM],
        out_specs=(VMEM,) * 2,
        scratch_shapes=[
            pltpu.VMEM((16, 2048), BF16),
            pltpu.VMEM((SLOTS, 2048), BF16),
            pltpu.VMEM((2048, 128), BF16),
            pltpu.VMEM((256, 2048), BF16),
            pltpu.VMEM((2048, 768), BF16),
            pltpu.SemaphoreType.DMA((12,)),
        ],
        compiler_params=params(11700),
    )(users, everyone, task, pair, cross_u, cross_v, cross_bias[None, :], gate_rows, expert_w, swap(expert_w))
    back = lax.all_to_all(part, CHIPS, 0, 0, tiled=True)
    score = pl.pallas_call(
        home_kernel,
        out_shape=jax.ShapeDtypeStruct((1, 32), F32),
        in_specs=[VMEM] * 3,
        out_specs=VMEM,
        compiler_params=params(12288),
    )(back, gates, owner)
    return score[0]


def solution(mesh):
    fine = Mesh(mesh.devices.reshape(mesh.devices.shape[0], 8, 2, 2, 2), ("grp", "z", "xl", "xh", "c"))
    t = ("z", "xl", "xh", "c")
    in_specs = (
        P("grp", t),
        P(None, t),
        P(None, t),
        P(t, None),
        P(t),
        P(t, None),
        P(("grp",) + t, None),
        P(("grp",) + t),
        P(("grp",) + t),
        P(),
        P(),
        P(),
        P(),
        P(None, None, t),
        P(None, None, t),
    )
    return jax.shard_map(body, mesh=fine, in_specs=in_specs, out_specs=P(("grp",) + t), check_vma=False)
```

```python
import math

import jax
import jax.numpy as jnp
from jax import lax
from jax.experimental import pallas as pl
from jax.experimental.pallas import tpu as pltpu
from jax.sharding import Mesh, PartitionSpec as P

D = 4096
EXPERTS = 3
TASKS = 4
REQ_GRP = 4
HIST = 32
epsilon = 1e-05

CHIPS = ("zh", "zl", "xh", "xl")
ALL = ("zh", "zl", "xh", "xl", "c")
HOLDERS = ("zh", "xh", "xl")
N_CHIPS = 32
F32 = jnp.float32
BF16 = jnp.bfloat16
HIGH = lax.Precision.HIGHEST

VMEM = pl.BlockSpec(memory_space=pltpu.VMEM)
ANY = pl.BlockSpec(memory_space=pl.ANY)
HBM = pl.BlockSpec(memory_space=pltpu.HBM)
ROW_BY_ROW = (((1,), (1,)), ((), ()))


def params(room_kib):
    return pltpu.CompilerParams(vmem_limit_bytes=(64 << 20) - (room_kib << 10))


def block_of(chip):
    return (chip & ~3) | ((chip & 1) << 1) | ((chip >> 1) & 1)


def split2(x):
    high = x.astype(BF16).astype(F32)
    return high, x - high


def lanes(shape):
    return lax.broadcasted_iota(jnp.int32, shape, len(shape) - 1)


def rows(shape):
    return lax.broadcasted_iota(jnp.int32, shape, len(shape) - 2)


def token_sums(x):
    padded = jnp.concatenate([x, jnp.zeros((128 - x.shape[0], 128), F32)], axis=0)
    return lax.dot_general(jnp.ones((8, 128), F32), padded, ROW_BY_ROW, precision=HIGH, preferred_element_type=F32)


def turn(x, by):
    return pltpu.roll(jnp.broadcast_to(x, (8, 128)), by, 1)[0:1]


def widen(x):
    return jnp.concatenate([x, jnp.zeros((1, 128 - x.shape[1]), x.dtype)], axis=1)


def pack_kernel(hist_ref, gain_ref, query_ref, head_ref, out_ref):
    hist = hist_ref[...].astype(F32)
    out_ref[0:128, :] = jnp.concatenate([hist, jnp.zeros((64, 128), F32)], axis=0).T.astype(BF16)
    row = rows((16, 128))
    ends = jnp.concatenate([gain_ref[...].astype(F32), query_ref[...].astype(F32)], axis=1)
    out_ref[128:144, :] = jnp.where(row == 0, ends, 0.0).astype(BF16)
    heads = jnp.zeros((16, 128), F32)
    for k in range(EXPERTS):
        head = head_ref[k].astype(F32)
        for t in range(TASKS):
            heads = jnp.where(row == t * EXPERTS + k, head[t : t + 1], heads)
    out_ref[144:160, :] = heads.astype(BF16)


def spread_kernel(pair_ref, out_ref, hist_ref, query_ref):
    core = lax.axis_index("c")
    tokens = pl.ds(pl.multiple_of(core * 64, 64), 64)
    first = pair_ref[0, tokens, :].astype(F32)
    second = pair_ref[1, tokens, :].astype(F32)
    hist = jnp.where(lanes((64, 128)) < 64, first, pltpu.roll(second, 64, 1))
    head0 = pair_ref[0, 128:144, :].astype(F32)[0:1]
    head1 = pair_ref[1, 128:144, :].astype(F32)[0:1]
    low = lanes((1, 128)) < 64
    gain = jnp.where(low, head0, turn(head1, 64))
    query = jnp.where(low, turn(head0, 64), head1)
    scaled = (hist * gain).astype(BF16)
    high, rest = split2(token_sums(hist * hist))
    row = rows((8, 128))
    extra = jnp.where(row == 0, high, jnp.where(row == 1, rest, 0.0)).astype(BF16)
    for chip in range(N_CHIPS):
        out_ref[chip, 0:64, :] = scaled
        out_ref[chip, 64:72, :] = extra
    hist_ref[...] = hist.astype(BF16)
    query_ref[...] = jnp.broadcast_to(query, (8, 128))


def tower_kernel(got_ref, up0_ref, up1_ref, down0_ref, down1_ref, out_ref, down, sems):
    copies = []
    for i, source in enumerate((down0_ref, down1_ref)):
        copies.append(pltpu.make_async_copy(source, down.at[128 * i : 128 * i + 128, :], sems.at[i]))
    for copy in copies:
        copy.start()
    stats = jnp.zeros((8, 128), F32)
    for chip in range(N_CHIPS):
        stats = stats + got_ref[chip, 64:72, :].astype(F32)
    inverse = lax.rsqrt((stats[0:1] + stats[1:2]) / D + epsilon)
    column = jnp.broadcast_to(inverse, (128, 128)).T[0:64]
    left = jnp.concatenate([got_ref[block_of(b), 0:64, :] for b in range(N_CHIPS)], axis=1)
    total = jnp.concatenate(
        [jnp.dot(left, up[...], preferred_element_type=F32) for up in (up0_ref, up1_ref)], axis=1
    )
    hidden = jax.nn.gelu(total * jnp.concatenate([column, column], axis=1)).astype(BF16)
    for copy in copies:
        copy.wait()
    part = jnp.dot(hidden, down[...], preferred_element_type=F32).astype(BF16)
    for b in range(N_CHIPS):
        out_ref[block_of(b), :, :] = part[:, 128 * b : 128 * b + 128]


def values_kernel(got_ref, hist_ref, query_ref, proj0_ref, proj1_ref, out_ref, proj, sems):
    copies = []
    for i, source in enumerate((proj0_ref, proj1_ref)):
        copies.append(pltpu.make_async_copy(source, proj.at[64 * i : 64 * i + 64, :], sems.at[i]))
    for copy in copies:
        copy.start()
    core = lax.axis_index("c")
    summed = got_ref[0].astype(F32)
    for chip in range(1, N_CHIPS):
        summed = summed + got_ref[chip].astype(F32)
    tower = (hist_ref[...].astype(F32) + summed).astype(BF16).astype(F32)
    square_high, square_rest = split2(token_sums(tower * tower))
    dot_high, dot_rest = split2(token_sums(tower * query_ref[0:1, :]))
    row = rows((8, 128))
    extra = jnp.where(row == 2, dot_high, jnp.where(row == 3, dot_rest, 0.0))
    extra = jnp.where(row == 0, square_high, jnp.where(row == 1, square_rest, extra)).astype(BF16)
    mine = jnp.where(core == 0, tower, pltpu.roll(tower, 64, 1)).astype(BF16)
    low = lanes((32, 128)) < 64
    for copy in copies:
        copy.wait()
    for j in range(16):
        part = jnp.dot(mine, proj[:, 128 * j : 128 * j + 128], preferred_element_type=F32)
        turned = pltpu.roll(part, 64, 1)
        out_ref[2 * j, 0:32, :] = jnp.where(low, part[0:32], turned[32:64]).astype(BF16)
        out_ref[2 * j + 1, 0:32, :] = jnp.where(low, turned[0:32], part[32:64]).astype(BF16)
        out_ref[2 * j, 32:40, :] = extra
        out_ref[2 * j + 1, 32:40, :] = extra


def user_kernel(got_ref, owner_ref, task_ref, out_ref):
    values = got_ref[0, 0:32, :].astype(F32)
    stats = got_ref[0, 32:40, :].astype(F32)
    for chip in range(1, N_CHIPS):
        values = values + got_ref[chip, 0:32, :].astype(F32)
        stats = stats + got_ref[chip, 32:40, :].astype(F32)
    squares = stats[0:1] + stats[1:2]
    dotted = stats[2:3] + stats[3:4]
    weight = jax.nn.sigmoid(dotted * lax.rsqrt(squares / D + epsilon))
    column = jnp.broadcast_to(weight, (128, 128)).T
    weights = jnp.where(lanes((32, 128)) < 64, column[0:32], column[32:64])
    user = jnp.sum(weights * values, axis=0, keepdims=True) / math.sqrt(HIST)
    slots = widen(owner_ref[...].astype(F32)) + turn(widen(task_ref[...].astype(F32)), 32)
    slots = slots + turn(slots, 64)
    out_ref[...] = jnp.where(rows((128, 128)) % 2 == 0, user, slots)


SLOTS = 512
STEP = 256


def score_kernel(
    got_ref, cand_ref, own_task_ref, pair_ref, near_ref, cross_u_ref, cross_v_ref, bias_ref, gate_ref, w0_ref, w1_ref,
    w2_ref, w3_ref, out_ref, gates_ref, users, x, cross_u, cross_v, w, sems,
):
    core = lax.axis_index("c")
    zl = lax.axis_index("zl")
    place = lax.axis_index("zh") * 4 + lax.axis_index("xh") * 2 + lax.axis_index("xl")

    def piece(i):
        part = slice(STEP * i, STEP * i + STEP)
        return pltpu.make_async_copy(cand_ref.at[part, :], x.at[part, :], sems.at[i])

    arrivals = [piece(i) for i in range(2)]
    get_u = pltpu.make_async_copy(cross_u_ref, cross_u, sems.at[4])
    get_v = pltpu.make_async_copy(cross_v_ref, cross_v.at[0:128, :], sems.at[5])
    get_w = []
    for k in range(EXPERTS):
        for i, source in enumerate((w0_ref, w1_ref, w2_ref, w3_ref)):
            start = 512 * k + 128 * i
            get_w.append(pltpu.make_async_copy(source.at[k], w.at[:, start : start + 128], sems.at[6 + 4 * k + i]))
    for copy in (arrivals[0], get_u, get_v, *arrivals[1:], *get_w):
        copy.start()
    row = rows((16, 128))
    low_half = lanes((1, 128)) < 64
    for j in range(16):
        full = jnp.zeros((16, 128), F32)
        for c in range(2):
            first = got_ref[8 * j + 2 * c : 8 * j + 2 * c + 1, :]
            second = got_ref[8 * j + 4 + 2 * c : 8 * j + 5 + 2 * c, :]
            full = jnp.where(row % 4 == 2 * c, jnp.where(low_half, first, turn(second, 64)), full)
            full = jnp.where(row % 4 == 2 * c + 1, jnp.where(low_half, turn(first, 64), second), full)
        high, rest = split2(full)
        mid, last = split2(rest)
        users[:, 128 * j : 128 * j + 128] = jnp.where(
            row < 4, high, jnp.where(row < 8, mid, jnp.where(row < 12, last, 0.0))
        ).astype(BF16)
    quarter = lanes((1, 128)) // 32
    owners, tasks = [], []
    for b in range(4):
        owner = jnp.zeros((1, 128), F32)
        task = jnp.zeros((1, 128), F32)
        for q in range(4):
            slots = got_ref[pl.ds(4 * (8 * b + 4 * zl + q) + 2 * core + 1, 1), :]
            turned = turn(slots, 32)
            owner = jnp.where(quarter == q, (slots, turned)[q % 2], owner)
            task = jnp.where(quarter == q, (turned, slots)[q % 2], task)
        owners.append(owner)
        tasks.append(task)
    owners = jnp.concatenate(owners, axis=1)
    tasks = jnp.concatenate(tasks, axis=1)
    heads = jnp.concatenate(
        [ref[which, 144:160, :] for ref in (pair_ref, near_ref) for which in (core, 1 - core)], axis=1
    )
    row = rows((16, 2048))
    bias = bias_ref[...].astype(F32)
    cross_v[128:144, :] = jnp.where(row == 0, bias, jnp.where(row == 1, 1.0, 0.0)).astype(BF16)
    cross_v[144:256, :] = jnp.zeros((112, 2048), BF16)
    ones = jnp.where(lanes((STEP, 128)) < 2, 1.0, 0.0).astype(BF16)
    row = rows((16, STEP))
    for i in range(2):
        part = slice(STEP * i, STEP * i + STEP)
        hot = jnp.where((row % 4).astype(F32) == owners[:, part], 1.0, 0.0).T.astype(BF16)
        arrivals[i].wait()
        if i == 0:
            get_u.wait()
        low = jnp.zeros((STEP, 128), F32)
        for j in range(8):
            cols = slice(256 * j, 256 * j + 256)
            added = jnp.dot(hot, users[:, cols], preferred_element_type=F32)
            x0 = (x[part, cols].astype(F32) + added).astype(BF16)
            x[part, cols] = x0
            low = low + jnp.dot(x0, cross_u[cols, :], preferred_element_type=F32)
        left = jnp.concatenate([low.astype(BF16), ones], axis=1)
        if i == 0:
            get_v.wait()
        for j in range(8):
            cols = slice(256 * j, 256 * j + 256)
            cross = jnp.dot(left, cross_v[:, cols], preferred_element_type=F32)
            x[part, cols] = (x[part, cols].astype(F32) * cross).astype(BF16)
    own = x[pl.ds(pl.multiple_of(place * 32, 32), 32), :]
    logits = lax.dot_general(gate_ref[...], own, ROW_BY_ROW, preferred_element_type=F32)
    row = rows((16, 32))
    picked = jnp.where(row // EXPERTS == own_task_ref[...], jax.nn.sigmoid(logits), 0.0)
    gates = picked / jnp.sum(picked, axis=0, keepdims=True)
    row_of = jnp.zeros((1, 128), F32)
    for k in range(EXPERTS):
        gate = widen(jnp.sum(jnp.where(row % EXPERTS == k, gates, 0.0), axis=0, keepdims=True))
        row_of = row_of + (gate if k == 0 else turn(gate, 32 * k))
    gates_ref[...] = row_of
    row = rows((16, SLOTS)).astype(F32)
    outs = []
    for k in range(EXPERTS):
        for copy in get_w[4 * k : 4 * k + 4]:
            copy.wait()
        active = jnp.dot(x[...], w[:, 512 * k : 512 * k + 512], preferred_element_type=F32)
        active = jax.nn.relu(active).astype(BF16)
        terms = lax.dot_general(heads, active, ROW_BY_ROW, preferred_element_type=F32)
        outs.append(jnp.sum(jnp.where(row == tasks * EXPERTS + k, terms, 0.0), axis=0, keepdims=True))
    for b in range(4):
        stack = jnp.concatenate([o[:, 128 * b : 128 * b + 128] for o in outs] + [jnp.zeros((5, 128), F32)], axis=0)
        turns = [stack] + [pltpu.roll(stack, 32 * q, 1) for q in range(1, 4)]
        for q in range(4):
            message = jnp.zeros((1, 128), F32)
            for k in range(EXPERTS):
                message = jnp.where(quarter == k, turns[(k - q) % 4][k : k + 1], message)
            out_ref[4 * b + q : 4 * b + q + 1, :] = message


def home_kernel(got_ref, gates_ref, owner_ref, out_ref):
    total = jnp.sum(got_ref[...], axis=0, keepdims=True) * gates_ref[...]
    total = total + turn(total, 64)
    total = total + turn(total, 32)
    out_ref[...] = jnp.where(owner_ref[...] < REQ_GRP, total[:, 0:32], 0.0)


def body(
    hist, tower_gain, up_w, down_w, query, proj_w, cand, owner, task, cross_u, cross_v, cross_bias, gate_w, expert_w, head_w,
):
    owner, task = owner[None, :], task[None, :]
    everyone = lax.all_gather(cand, HOLDERS, axis=0, tiled=True)
    message = pl.pallas_call(
        pack_kernel,
        out_shape=jax.ShapeDtypeStruct((160, 128), BF16),
        in_specs=[VMEM] * 4,
        out_specs=VMEM,
        compiler_params=params(64),
    )(hist.T, tower_gain, query[None, :], head_w.transpose(1, 0, 2))
    pair = lax.all_gather(message, "c", axis=0)
    spread, hist_c, query_c = pl.pallas_call(
        spread_kernel,
        out_shape=(
            jax.ShapeDtypeStruct((N_CHIPS, 72, 128), BF16),
            jax.ShapeDtypeStruct((64, 128), BF16),
            jax.ShapeDtypeStruct((8, 128), F32),
        ),
        in_specs=[VMEM],
        out_specs=(VMEM,) * 3,
        compiler_params=params(63 << 10),
    )(pair)
    tokens = lax.all_to_all(spread, CHIPS, 0, 0, tiled=True)
    swap = lambda x: lax.ppermute(x, "c", [(0, 1), (1, 0)])
    parts = pl.pallas_call(
        tower_kernel,
        out_shape=jax.ShapeDtypeStruct((N_CHIPS, 64, 128), BF16),
        in_specs=[VMEM] * 3 + [HBM] * 2,
        out_specs=VMEM,
        scratch_shapes=[pltpu.VMEM((256, 4096), BF16), pltpu.SemaphoreType.DMA((2,))],
        compiler_params=params(13900),
    )(tokens, up_w, swap(up_w), down_w, swap(down_w))
    summed = lax.all_to_all(parts, CHIPS, 0, 0, tiled=True)
    values = pl.pallas_call(
        values_kernel,
        out_shape=jax.ShapeDtypeStruct((N_CHIPS, 40, 128), BF16),
        in_specs=[VMEM] * 3 + [HBM] * 2,
        out_specs=VMEM,
        scratch_shapes=[pltpu.VMEM((128, 2048), BF16), pltpu.SemaphoreType.DMA((2,))],
        compiler_params=params(12160),
    )(summed, hist_c, query_c, proj_w, swap(proj_w))
    values = lax.all_to_all(values, CHIPS, 0, 0, tiled=True)
    user = pl.pallas_call(
        user_kernel,
        out_shape=jax.ShapeDtypeStruct((128, 128), F32),
        in_specs=[VMEM] * 3,
        out_specs=VMEM,
        compiler_params=params(12288),
    )(values, owner, task)
    users = lax.all_to_all(user, ALL, 0, 0, tiled=True)
    near = lambda x: lax.ppermute(x, "zl", [(0, 1), (1, 0)])
    expert_near = near(expert_w)
    gate_rows = jnp.pad(gate_w.T, ((0, 4), (0, 0)))
    part, gates = pl.pallas_call(
        score_kernel,
        out_shape=(jax.ShapeDtypeStruct((16, 128), F32), jax.ShapeDtypeStruct((1, 128), F32)),
        in_specs=[VMEM, HBM, VMEM, VMEM, VMEM, HBM, HBM, VMEM, VMEM, HBM, HBM, HBM, HBM],
        out_specs=(VMEM,) * 2,
        scratch_shapes=[
            pltpu.VMEM((16, 2048), BF16),
            pltpu.VMEM((SLOTS, 2048), BF16),
            pltpu.VMEM((2048, 128), BF16),
            pltpu.VMEM((256, 2048), BF16),
            pltpu.VMEM((2048, 1536), BF16),
            pltpu.SemaphoreType.DMA((18,)),
        ],
        compiler_params=params(11900),
    )(
        users, everyone, task, pair, near(pair), cross_u, cross_v, cross_bias[None, :], gate_rows,
        expert_w, swap(expert_w), expert_near, swap(expert_near),
    )
    back = lax.all_to_all(part, HOLDERS, 0, 0, tiled=True)
    score = pl.pallas_call(
        home_kernel,
        out_shape=jax.ShapeDtypeStruct((1, 32), F32),
        in_specs=[VMEM] * 3,
        out_specs=VMEM,
        compiler_params=params(12288),
    )(back, gates, owner)
    return score[0]


def solution(mesh):
    fine = Mesh(mesh.devices.reshape(mesh.devices.shape[0], 4, 2, 2, 2, 2), ("grp", "zh", "zl", "xl", "xh", "c"))
    t = ("zh", "zl", "xl", "xh", "c")
    in_specs = (
        P("grp", t),
        P(None, t),
        P(None, t),
        P(t, None),
        P(t),
        P(t, None),
        P(("grp",) + t, None),
        P(("grp",) + t),
        P(("grp",) + t),
        P(),
        P(),
        P(),
        P(),
        P(None, None, t),
        P(None, None, t),
    )
    return jax.shard_map(body, mesh=fine, in_specs=in_specs, out_specs=P(("grp",) + t), check_vma=False)
```

```python
import math

import jax
import jax.numpy as jnp
from jax import lax
from jax.experimental import pallas as pl
from jax.experimental.pallas import tpu as pltpu
from jax.sharding import Mesh, PartitionSpec as P

D = 4096
EXPERTS = 3
TASKS = 4
REQ_GRP = 4
HIST = 32
epsilon = 1e-05

CHIPS = ("z", "xh", "xl")
ALL = ("z", "xh", "xl", "c")
N_CHIPS = 32
F32 = jnp.float32
BF16 = jnp.bfloat16
HIGH = lax.Precision.HIGHEST

VMEM = pl.BlockSpec(memory_space=pltpu.VMEM)
ANY = pl.BlockSpec(memory_space=pl.ANY)
HBM = pl.BlockSpec(memory_space=pltpu.HBM)
ROW_BY_ROW = (((1,), (1,)), ((), ()))


def params(room_kib):
    return pltpu.CompilerParams(vmem_limit_bytes=(64 << 20) - (room_kib << 10))


def block_of(chip):
    return (chip & ~3) | ((chip & 1) << 1) | ((chip >> 1) & 1)


def split2(x):
    high = x.astype(BF16).astype(F32)
    return high, x - high


def lanes(shape):
    return lax.broadcasted_iota(jnp.int32, shape, len(shape) - 1)


def rows(shape):
    return lax.broadcasted_iota(jnp.int32, shape, len(shape) - 2)


def token_sums(x):
    padded = jnp.concatenate([x, jnp.zeros((128 - x.shape[0], 128), F32)], axis=0)
    return lax.dot_general(jnp.ones((8, 128), F32), padded, ROW_BY_ROW, precision=HIGH, preferred_element_type=F32)


def turn(x, by):
    return pltpu.roll(jnp.broadcast_to(x, (8, 128)), by, 1)[0:1]


def widen(x):
    return jnp.concatenate([x, jnp.zeros((1, 128 - x.shape[1]), x.dtype)], axis=1)


def pack_kernel(hist_ref, gain_ref, query_ref, head_ref, out_ref):
    hist = hist_ref[...].astype(F32)
    out_ref[0:128, :] = jnp.concatenate([hist, jnp.zeros((64, 128), F32)], axis=0).T.astype(BF16)
    row = rows((16, 128))
    ends = jnp.concatenate([gain_ref[...].astype(F32), query_ref[...].astype(F32)], axis=1)
    out_ref[128:144, :] = jnp.where(row == 0, ends, 0.0).astype(BF16)
    heads = jnp.zeros((16, 128), F32)
    for k in range(EXPERTS):
        head = head_ref[k].astype(F32)
        for t in range(TASKS):
            heads = jnp.where(row == t * EXPERTS + k, head[t : t + 1], heads)
    out_ref[144:160, :] = heads.astype(BF16)


def spread_kernel(pair_ref, out_ref, hist_ref, query_ref):
    core = lax.axis_index("c")
    tokens = pl.ds(pl.multiple_of(core * 64, 64), 64)
    first = pair_ref[0, tokens, :].astype(F32)
    second = pair_ref[1, tokens, :].astype(F32)
    hist = jnp.where(lanes((64, 128)) < 64, first, pltpu.roll(second, 64, 1))
    head0 = pair_ref[0, 128:144, :].astype(F32)[0:1]
    head1 = pair_ref[1, 128:144, :].astype(F32)[0:1]
    low = lanes((1, 128)) < 64
    gain = jnp.where(low, head0, turn(head1, 64))
    query = jnp.where(low, turn(head0, 64), head1)
    scaled = (hist * gain).astype(BF16)
    high, rest = split2(token_sums(hist * hist))
    row = rows((8, 128))
    extra = jnp.where(row == 0, high, jnp.where(row == 1, rest, 0.0)).astype(BF16)
    for chip in range(N_CHIPS):
        out_ref[chip, 0:64, :] = scaled
        out_ref[chip, 64:72, :] = extra
    hist_ref[...] = hist.astype(BF16)
    query_ref[...] = jnp.broadcast_to(query, (8, 128))


def tower_kernel(got_ref, up0_ref, up1_ref, down0_ref, down1_ref, out_ref, down, sems):
    copies = []
    for i, source in enumerate((down0_ref, down1_ref)):
        copies.append(pltpu.make_async_copy(source, down.at[128 * i : 128 * i + 128, :], sems.at[i]))
    for copy in copies:
        copy.start()
    stats = jnp.zeros((8, 128), F32)
    for chip in range(N_CHIPS):
        stats = stats + got_ref[chip, 64:72, :].astype(F32)
    inverse = lax.rsqrt((stats[0:1] + stats[1:2]) / D + epsilon)
    column = jnp.broadcast_to(inverse, (128, 128)).T[0:64]
    left = jnp.concatenate([got_ref[block_of(b), 0:64, :] for b in range(N_CHIPS)], axis=1)
    total = jnp.concatenate(
        [jnp.dot(left, up[...], preferred_element_type=F32) for up in (up0_ref, up1_ref)], axis=1
    )
    hidden = jax.nn.gelu(total * jnp.concatenate([column, column], axis=1)).astype(BF16)
    for copy in copies:
        copy.wait()
    part = jnp.dot(hidden, down[...], preferred_element_type=F32).astype(BF16)
    for b in range(N_CHIPS):
        out_ref[block_of(b), :, :] = part[:, 128 * b : 128 * b + 128]


def values_kernel(got_ref, hist_ref, query_ref, proj0_ref, proj1_ref, out_ref, proj, sems):
    copies = []
    for i, source in enumerate((proj0_ref, proj1_ref)):
        copies.append(pltpu.make_async_copy(source, proj.at[64 * i : 64 * i + 64, :], sems.at[i]))
    for copy in copies:
        copy.start()
    core = lax.axis_index("c")
    summed = got_ref[0].astype(F32)
    for chip in range(1, N_CHIPS):
        summed = summed + got_ref[chip].astype(F32)
    tower = (hist_ref[...].astype(F32) + summed).astype(BF16).astype(F32)
    square_high, square_rest = split2(token_sums(tower * tower))
    dot_high, dot_rest = split2(token_sums(tower * query_ref[0:1, :]))
    row = rows((8, 128))
    extra = jnp.where(row == 2, dot_high, jnp.where(row == 3, dot_rest, 0.0))
    extra = jnp.where(row == 0, square_high, jnp.where(row == 1, square_rest, extra)).astype(BF16)
    mine = jnp.where(core == 0, tower, pltpu.roll(tower, 64, 1)).astype(BF16)
    low = lanes((32, 128)) < 64
    for copy in copies:
        copy.wait()
    for j in range(16):
        part = jnp.dot(mine, proj[:, 128 * j : 128 * j + 128], preferred_element_type=F32)
        turned = pltpu.roll(part, 64, 1)
        out_ref[2 * j, 0:32, :] = jnp.where(low, part[0:32], turned[32:64]).astype(BF16)
        out_ref[2 * j + 1, 0:32, :] = jnp.where(low, turned[0:32], part[32:64]).astype(BF16)
        out_ref[2 * j, 32:40, :] = extra
        out_ref[2 * j + 1, 32:40, :] = extra


def user_kernel(got_ref, owner_ref, task_ref, out_ref):
    values = got_ref[0, 0:32, :].astype(F32)
    stats = got_ref[0, 32:40, :].astype(F32)
    for chip in range(1, N_CHIPS):
        values = values + got_ref[chip, 0:32, :].astype(F32)
        stats = stats + got_ref[chip, 32:40, :].astype(F32)
    squares = stats[0:1] + stats[1:2]
    dotted = stats[2:3] + stats[3:4]
    weight = jax.nn.sigmoid(dotted * lax.rsqrt(squares / D + epsilon))
    column = jnp.broadcast_to(weight, (128, 128)).T
    weights = jnp.where(lanes((32, 128)) < 64, column[0:32], column[32:64])
    user = jnp.sum(weights * values, axis=0, keepdims=True) / math.sqrt(HIST)
    slots = widen(owner_ref[...].astype(F32)) + turn(widen(task_ref[...].astype(F32)), 32)
    slots = slots + turn(slots, 64)
    out_ref[...] = jnp.where(rows((128, 128)) % 2 == 0, user, slots)


SLOTS = 1024
STEP = 256


def score_kernel(
    got_ref, cand_ref, own_task_ref, pair_ref, cross_u_ref, cross_v_ref, bias_ref, gate_ref, w0_ref, w1_ref,
    out_ref, gates_ref, users, x, cross_u, cross_v, w, sems,
):
    core = lax.axis_index("c")
    chip_here = lax.axis_index("z") * 4 + lax.axis_index("xh") * 2 + lax.axis_index("xl")

    def piece(i):
        part = slice(STEP * i, STEP * i + STEP)
        return pltpu.make_async_copy(cand_ref.at[part, :], x.at[part, :], sems.at[i])

    arrivals = [piece(i) for i in range(4)]
    get_u = pltpu.make_async_copy(cross_u_ref, cross_u, sems.at[4])
    get_v = pltpu.make_async_copy(cross_v_ref, cross_v.at[0:128, :], sems.at[5])
    get_w = []
    for k in range(EXPERTS):
        for i, source in enumerate((w0_ref, w1_ref)):
            start = 256 * k + 128 * i
            get_w.append(pltpu.make_async_copy(source.at[k], w.at[:, start : start + 128], sems.at[6 + 2 * k + i]))
    for copy in (arrivals[0], get_u, get_v, *arrivals[1:], *get_w):
        copy.start()
    row = rows((16, 128))
    low_half = lanes((1, 128)) < 64
    for j in range(16):
        full = jnp.zeros((16, 128), F32)
        for c in range(2):
            first = got_ref[8 * j + 2 * c : 8 * j + 2 * c + 1, :]
            second = got_ref[8 * j + 4 + 2 * c : 8 * j + 5 + 2 * c, :]
            full = jnp.where(row % 4 == 2 * c, jnp.where(low_half, first, turn(second, 64)), full)
            full = jnp.where(row % 4 == 2 * c + 1, jnp.where(low_half, turn(first, 64), second), full)
        high, rest = split2(full)
        mid, last = split2(rest)
        users[:, 128 * j : 128 * j + 128] = jnp.where(
            row < 4, high, jnp.where(row < 8, mid, jnp.where(row < 12, last, 0.0))
        ).astype(BF16)
    quarter = lanes((1, 128)) // 32
    owners, tasks = [], []
    for b in range(8):
        owner = jnp.zeros((1, 128), F32)
        task = jnp.zeros((1, 128), F32)
        for q in range(4):
            slots = got_ref[pl.ds(4 * (4 * b + q) + 2 * core + 1, 1), :]
            turned = turn(slots, 32)
            owner = jnp.where(quarter == q, (slots, turned)[q % 2], owner)
            task = jnp.where(quarter == q, (turned, slots)[q % 2], task)
        owners.append(owner)
        tasks.append(task)
    owners = jnp.concatenate(owners, axis=1)
    tasks = jnp.concatenate(tasks, axis=1)
    heads = jnp.concatenate([pair_ref[core, 144:160, :], pair_ref[1 - core, 144:160, :]], axis=1)
    row = rows((16, 2048))
    bias = bias_ref[...].astype(F32)
    cross_v[128:144, :] = jnp.where(row == 0, bias, jnp.where(row == 1, 1.0, 0.0)).astype(BF16)
    cross_v[144:256, :] = jnp.zeros((112, 2048), BF16)
    ones = jnp.where(lanes((STEP, 128)) < 2, 1.0, 0.0).astype(BF16)
    row = rows((16, STEP))
    for i in range(4):
        part = slice(STEP * i, STEP * i + STEP)
        hot = jnp.where((row % 4).astype(F32) == owners[:, part], 1.0, 0.0).T.astype(BF16)
        arrivals[i].wait()
        if i == 0:
            get_u.wait()
        for j in range(8):
            cols = slice(256 * j, 256 * j + 256)
            added = jnp.dot(hot, users[:, cols], preferred_element_type=F32)
            x[part, cols] = (x[part, cols].astype(F32) + added).astype(BF16)
        low = jnp.dot(x[part, :], cross_u[...], preferred_element_type=F32)
        left = jnp.concatenate([low.astype(BF16), ones], axis=1)
        if i == 0:
            get_v.wait()
        for j in range(8):
            cols = slice(256 * j, 256 * j + 256)
            cross = jnp.dot(left, cross_v[:, cols], preferred_element_type=F32)
            x[part, cols] = (x[part, cols].astype(F32) * cross).astype(BF16)
    own = x[pl.ds(pl.multiple_of(chip_here * 32, 32), 32), :]
    logits = lax.dot_general(gate_ref[...], own, ROW_BY_ROW, preferred_element_type=F32)
    row = rows((16, 32))
    picked = jnp.where(row // EXPERTS == own_task_ref[...], jax.nn.sigmoid(logits), 0.0)
    gates = picked / jnp.sum(picked, axis=0, keepdims=True)
    row_of = jnp.zeros((1, 128), F32)
    for k in range(EXPERTS):
        gate = widen(jnp.sum(jnp.where(row % EXPERTS == k, gates, 0.0), axis=0, keepdims=True))
        row_of = row_of + (gate if k == 0 else turn(gate, 32 * k))
    gates_ref[...] = row_of
    for copy in get_w:
        copy.wait()
    active = jax.nn.relu(jnp.dot(x[...], w[...], preferred_element_type=F32)).astype(BF16)
    row = rows((16, SLOTS)).astype(F32)
    outs = []
    for k in range(EXPERTS):
        terms = lax.dot_general(heads, active[:, 256 * k : 256 * k + 256], ROW_BY_ROW, preferred_element_type=F32)
        outs.append(jnp.sum(jnp.where(row == tasks * EXPERTS + k, terms, 0.0), axis=0, keepdims=True))
    for b in range(8):
        stack = jnp.concatenate([o[:, 128 * b : 128 * b + 128] for o in outs] + [jnp.zeros((5, 128), F32)], axis=0)
        turns = [stack] + [pltpu.roll(stack, 32 * q, 1) for q in range(1, 4)]
        for q in range(4):
            message = jnp.zeros((1, 128), F32)
            for k in range(EXPERTS):
                message = jnp.where(quarter == k, turns[(k - q) % 4][k : k + 1], message)
            out_ref[4 * b + q : 4 * b + q + 1, :] = message


def home_kernel(got_ref, gates_ref, owner_ref, out_ref):
    total = jnp.sum(got_ref[...], axis=0, keepdims=True) * gates_ref[...]
    total = total + turn(total, 64)
    total = total + turn(total, 32)
    out_ref[...] = jnp.where(owner_ref[...] < REQ_GRP, total[:, 0:32], 0.0)


def body(
    hist, tower_gain, up_w, down_w, query, proj_w, cand, owner, task, cross_u, cross_v, cross_bias, gate_w, expert_w, head_w,
):
    owner, task = owner[None, :], task[None, :]
    everyone = lax.all_gather(cand, CHIPS, axis=0, tiled=True)
    message = pl.pallas_call(
        pack_kernel,
        out_shape=jax.ShapeDtypeStruct((160, 128), BF16),
        in_specs=[VMEM] * 4,
        out_specs=VMEM,
        compiler_params=params(64),
    )(hist.T, tower_gain, query[None, :], head_w.transpose(1, 0, 2))
    pair = lax.all_gather(message, "c", axis=0)
    spread, hist_c, query_c = pl.pallas_call(
        spread_kernel,
        out_shape=(
            jax.ShapeDtypeStruct((N_CHIPS, 72, 128), BF16),
            jax.ShapeDtypeStruct((64, 128), BF16),
            jax.ShapeDtypeStruct((8, 128), F32),
        ),
        in_specs=[VMEM],
        out_specs=(VMEM,) * 3,
        compiler_params=params(63 << 10),
    )(pair)
    tokens = lax.all_to_all(spread, CHIPS, 0, 0, tiled=True)
    swap = lambda x: lax.ppermute(x, "c", [(0, 1), (1, 0)])
    parts = pl.pallas_call(
        tower_kernel,
        out_shape=jax.ShapeDtypeStruct((N_CHIPS, 64, 128), BF16),
        in_specs=[VMEM] * 3 + [HBM] * 2,
        out_specs=VMEM,
        scratch_shapes=[pltpu.VMEM((256, 4096), BF16), pltpu.SemaphoreType.DMA((2,))],
        compiler_params=params(13900),
    )(tokens, up_w, swap(up_w), down_w, swap(down_w))
    summed = lax.all_to_all(parts, CHIPS, 0, 0, tiled=True)
    values = pl.pallas_call(
        values_kernel,
        out_shape=jax.ShapeDtypeStruct((N_CHIPS, 40, 128), BF16),
        in_specs=[VMEM] * 3 + [HBM] * 2,
        out_specs=VMEM,
        scratch_shapes=[pltpu.VMEM((128, 2048), BF16), pltpu.SemaphoreType.DMA((2,))],
        compiler_params=params(12160),
    )(summed, hist_c, query_c, proj_w, swap(proj_w))
    values = lax.all_to_all(values, CHIPS, 0, 0, tiled=True)
    user = pl.pallas_call(
        user_kernel,
        out_shape=jax.ShapeDtypeStruct((128, 128), F32),
        in_specs=[VMEM] * 3,
        out_specs=VMEM,
        compiler_params=params(12288),
    )(values, owner, task)
    users = lax.all_to_all(user, ALL, 0, 0, tiled=True)
    gate_rows = jnp.pad(gate_w.T, ((0, 4), (0, 0)))
    part, gates = pl.pallas_call(
        score_kernel,
        out_shape=(jax.ShapeDtypeStruct((N_CHIPS, 128), F32), jax.ShapeDtypeStruct((1, 128), F32)),
        in_specs=[VMEM, HBM, VMEM, VMEM, HBM, HBM, VMEM, VMEM, HBM, HBM],
        out_specs=(VMEM,) * 2,
        scratch_shapes=[
            pltpu.VMEM((16, 2048), BF16),
            pltpu.VMEM((SLOTS, 2048), BF16),
            pltpu.VMEM((2048, 128), BF16),
            pltpu.VMEM((256, 2048), BF16),
            pltpu.VMEM((2048, 768), BF16),
            pltpu.SemaphoreType.DMA((12,)),
        ],
        compiler_params=params(11700),
    )(users, everyone, task, pair, cross_u, cross_v, cross_bias[None, :], gate_rows, expert_w, swap(expert_w))
    back = lax.all_to_all(part, CHIPS, 0, 0, tiled=True)
    score = pl.pallas_call(
        home_kernel,
        out_shape=jax.ShapeDtypeStruct((1, 32), F32),
        in_specs=[VMEM] * 3,
        out_specs=VMEM,
        compiler_params=params(12288),
    )(back, gates, owner)
    return score[0]


def solution(mesh):
    fine = Mesh(mesh.devices.reshape(mesh.devices.shape[0], 8, 2, 2, 2), ("grp", "z", "xl", "xh", "c"))
    t = ("z", "xl", "xh", "c")
    in_specs = (
        P("grp", t),
        P(None, t),
        P(None, t),
        P(t, None),
        P(t),
        P(t, None),
        P(("grp",) + t, None),
        P(("grp",) + t),
        P(("grp",) + t),
        P(),
        P(),
        P(),
        P(),
        P(None, None, t),
        P(None, None, t),
    )
    return jax.shard_map(body, mesh=fine, in_specs=in_specs, out_specs=P(("grp",) + t), check_vma=False)
```

```python
import math

import jax
import jax.numpy as jnp
from jax import lax
from jax.experimental import pallas as pl
from jax.experimental.pallas import tpu as pltpu
from jax.sharding import Mesh, PartitionSpec as P

D = 4096
EXPERTS = 3
TASKS = 4
REQ_GRP = 4
HIST = 32
epsilon = 1e-05

CHIPS = ("z", "xh", "xl")
ALL = ("z", "xh", "xl", "c")
N_CHIPS = 32
F32 = jnp.float32
BF16 = jnp.bfloat16
HIGH = lax.Precision.HIGHEST

VMEM = pl.BlockSpec(memory_space=pltpu.VMEM)
ANY = pl.BlockSpec(memory_space=pl.ANY)
HBM = pl.BlockSpec(memory_space=pltpu.HBM)
ROW_BY_ROW = (((1,), (1,)), ((), ()))


def params(room_kib):
    return pltpu.CompilerParams(vmem_limit_bytes=(64 << 20) - (room_kib << 10))


def block_of(chip):
    return (chip & ~3) | ((chip & 1) << 1) | ((chip >> 1) & 1)


def split2(x):
    high = x.astype(BF16).astype(F32)
    return high, x - high


def lanes(shape):
    return lax.broadcasted_iota(jnp.int32, shape, len(shape) - 1)


def rows(shape):
    return lax.broadcasted_iota(jnp.int32, shape, len(shape) - 2)


def token_sums(x):
    padded = jnp.concatenate([x, jnp.zeros((128 - x.shape[0], 128), F32)], axis=0)
    return lax.dot_general(jnp.ones((8, 128), F32), padded, ROW_BY_ROW, precision=HIGH, preferred_element_type=F32)


def turn(x, by):
    return pltpu.roll(jnp.broadcast_to(x, (8, 128)), by, 1)[0:1]


def widen(x):
    return jnp.concatenate([x, jnp.zeros((1, 128 - x.shape[1]), x.dtype)], axis=1)


def pack_kernel(hist_ref, gain_ref, query_ref, head_ref, out_ref):
    hist = hist_ref[...].astype(F32)
    out_ref[0:128, :] = jnp.concatenate([hist, jnp.zeros((64, 128), F32)], axis=0).T.astype(BF16)
    row = rows((16, 128))
    ends = jnp.concatenate([gain_ref[...].astype(F32), query_ref[...].astype(F32)], axis=1)
    out_ref[128:144, :] = jnp.where(row == 0, ends, 0.0).astype(BF16)
    heads = jnp.zeros((16, 128), F32)
    for k in range(EXPERTS):
        head = head_ref[k].astype(F32)
        for t in range(TASKS):
            heads = jnp.where(row == t * EXPERTS + k, head[t : t + 1], heads)
    out_ref[144:160, :] = heads.astype(BF16)


def spread_kernel(pair_ref, out_ref, hist_ref, query_ref):
    core = lax.axis_index("c")
    tokens = pl.ds(pl.multiple_of(core * 64, 64), 64)
    first = pair_ref[0, tokens, :].astype(F32)
    second = pair_ref[1, tokens, :].astype(F32)
    hist = jnp.where(lanes((64, 128)) < 64, first, pltpu.roll(second, 64, 1))
    head0 = pair_ref[0, 128:144, :].astype(F32)[0:1]
    head1 = pair_ref[1, 128:144, :].astype(F32)[0:1]
    low = lanes((1, 128)) < 64
    gain = jnp.where(low, head0, turn(head1, 64))
    query = jnp.where(low, turn(head0, 64), head1)
    scaled = (hist * gain).astype(BF16)
    high, rest = split2(token_sums(hist * hist))
    row = rows((8, 128))
    extra = jnp.where(row == 0, high, jnp.where(row == 1, rest, 0.0)).astype(BF16)
    for chip in range(N_CHIPS):
        out_ref[chip, 0:64, :] = scaled
        out_ref[chip, 64:72, :] = extra
    hist_ref[...] = hist.astype(BF16)
    query_ref[...] = jnp.broadcast_to(query, (8, 128))


def tower_kernel(got_ref, up0_ref, up1_ref, down0_ref, down1_ref, out_ref, down, sems):
    copies = []
    for i, source in enumerate((down0_ref, down1_ref)):
        copies.append(pltpu.make_async_copy(source, down.at[128 * i : 128 * i + 128, :], sems.at[i]))
    for copy in copies:
        copy.start()
    stats = jnp.zeros((8, 128), F32)
    for chip in range(N_CHIPS):
        stats = stats + got_ref[chip, 64:72, :].astype(F32)
    inverse = lax.rsqrt((stats[0:1] + stats[1:2]) / D + epsilon)
    column = jnp.broadcast_to(inverse, (128, 128)).T[0:64]
    left = jnp.concatenate([got_ref[block_of(b), 0:64, :] for b in range(N_CHIPS)], axis=1)
    total = jnp.concatenate(
        [jnp.dot(left, up[...], preferred_element_type=F32) for up in (up0_ref, up1_ref)], axis=1
    )
    hidden = jax.nn.gelu(total * jnp.concatenate([column, column], axis=1)).astype(BF16)
    for copy in copies:
        copy.wait()
    part = jnp.dot(hidden, down[...], preferred_element_type=F32).astype(BF16)
    for b in range(N_CHIPS):
        out_ref[block_of(b), :, :] = part[:, 128 * b : 128 * b + 128]


def values_kernel(got_ref, hist_ref, query_ref, proj0_ref, proj1_ref, out_ref, proj, sems):
    copies = []
    for i, source in enumerate((proj0_ref, proj1_ref)):
        copies.append(pltpu.make_async_copy(source, proj.at[64 * i : 64 * i + 64, :], sems.at[i]))
    for copy in copies:
        copy.start()
    core = lax.axis_index("c")
    summed = got_ref[0].astype(F32)
    for chip in range(1, N_CHIPS):
        summed = summed + got_ref[chip].astype(F32)
    tower = (hist_ref[...].astype(F32) + summed).astype(BF16).astype(F32)
    square_high, square_rest = split2(token_sums(tower * tower))
    dot_high, dot_rest = split2(token_sums(tower * query_ref[0:1, :]))
    row = rows((8, 128))
    extra = jnp.where(row == 2, dot_high, jnp.where(row == 3, dot_rest, 0.0))
    extra = jnp.where(row == 0, square_high, jnp.where(row == 1, square_rest, extra)).astype(BF16)
    mine = jnp.where(core == 0, tower, pltpu.roll(tower, 64, 1)).astype(BF16)
    low = lanes((32, 128)) < 64
    for copy in copies:
        copy.wait()
    for j in range(16):
        part = jnp.dot(mine, proj[:, 128 * j : 128 * j + 128], preferred_element_type=F32)
        turned = pltpu.roll(part, 64, 1)
        out_ref[2 * j, 0:32, :] = jnp.where(low, part[0:32], turned[32:64]).astype(BF16)
        out_ref[2 * j + 1, 0:32, :] = jnp.where(low, turned[0:32], part[32:64]).astype(BF16)
        out_ref[2 * j, 32:40, :] = extra
        out_ref[2 * j + 1, 32:40, :] = extra


def user_kernel(got_ref, owner_ref, task_ref, out_ref):
    values = got_ref[0, 0:32, :].astype(F32)
    stats = got_ref[0, 32:40, :].astype(F32)
    for chip in range(1, N_CHIPS):
        values = values + got_ref[chip, 0:32, :].astype(F32)
        stats = stats + got_ref[chip, 32:40, :].astype(F32)
    squares = stats[0:1] + stats[1:2]
    dotted = stats[2:3] + stats[3:4]
    weight = jax.nn.sigmoid(dotted * lax.rsqrt(squares / D + epsilon))
    column = jnp.broadcast_to(weight, (128, 128)).T
    weights = jnp.where(lanes((32, 128)) < 64, column[0:32], column[32:64])
    user = jnp.sum(weights * values, axis=0, keepdims=True) / math.sqrt(HIST)
    slots = widen(owner_ref[...].astype(F32)) + turn(widen(task_ref[...].astype(F32)), 32)
    slots = slots + turn(slots, 64)
    out_ref[...] = jnp.where(rows((128, 128)) % 2 == 0, user, slots)


SLOTS = 1024
STEP = 256


def score_kernel(
    got_ref, cand_ref, own_task_ref, pair_ref, cross_u_ref, cross_v_ref, bias_ref, gate_ref, w0_ref, w1_ref,
    out_ref, gates_ref, users, x, cross_u, cross_v, w, sems,
):
    core = lax.axis_index("c")
    chip_here = lax.axis_index("z") * 4 + lax.axis_index("xh") * 2 + lax.axis_index("xl")

    def piece(i):
        part = slice(STEP * i, STEP * i + STEP)
        return pltpu.make_async_copy(cand_ref.at[part, :], x.at[part, :], sems.at[i])

    arrivals = [piece(i) for i in range(4)]
    get_u = pltpu.make_async_copy(cross_u_ref, cross_u, sems.at[4])
    get_v = pltpu.make_async_copy(cross_v_ref, cross_v.at[0:128, :], sems.at[5])
    get_w = []
    for k in range(EXPERTS):
        for i, source in enumerate((w0_ref, w1_ref)):
            start = 256 * k + 128 * i
            get_w.append(pltpu.make_async_copy(source.at[k], w.at[:, start : start + 128], sems.at[6 + 2 * k + i]))
    for copy in (arrivals[0], get_u, get_v, *arrivals[1:]):
        copy.start()
    row = rows((16, 128))
    low_half = lanes((1, 128)) < 64
    for j in range(16):
        full = jnp.zeros((16, 128), F32)
        for c in range(2):
            first = got_ref[8 * j + 2 * c : 8 * j + 2 * c + 1, :]
            second = got_ref[8 * j + 4 + 2 * c : 8 * j + 5 + 2 * c, :]
            full = jnp.where(row % 4 == 2 * c, jnp.where(low_half, first, turn(second, 64)), full)
            full = jnp.where(row % 4 == 2 * c + 1, jnp.where(low_half, turn(first, 64), second), full)
        high, rest = split2(full)
        mid, last = split2(rest)
        users[:, 128 * j : 128 * j + 128] = jnp.where(
            row < 4, high, jnp.where(row < 8, mid, jnp.where(row < 12, last, 0.0))
        ).astype(BF16)
    quarter = lanes((1, 128)) // 32
    owners, tasks = [], []
    for b in range(8):
        owner = jnp.zeros((1, 128), F32)
        task = jnp.zeros((1, 128), F32)
        for q in range(4):
            slots = got_ref[pl.ds(4 * (4 * b + q) + 2 * core + 1, 1), :]
            turned = turn(slots, 32)
            owner = jnp.where(quarter == q, (slots, turned)[q % 2], owner)
            task = jnp.where(quarter == q, (turned, slots)[q % 2], task)
        owners.append(owner)
        tasks.append(task)
    owners = jnp.concatenate(owners, axis=1)
    tasks = jnp.concatenate(tasks, axis=1)
    heads = jnp.concatenate([pair_ref[core, 144:160, :], pair_ref[1 - core, 144:160, :]], axis=1)
    row = rows((16, 2048))
    bias = bias_ref[...].astype(F32)
    cross_v[128:144, :] = jnp.where(row == 0, bias, jnp.where(row == 1, 1.0, 0.0)).astype(BF16)
    cross_v[144:256, :] = jnp.zeros((112, 2048), BF16)
    ones = jnp.where(lanes((STEP, 128)) < 2, 1.0, 0.0).astype(BF16)
    row = rows((16, STEP))
    for i in range(4):
        part = slice(STEP * i, STEP * i + STEP)
        hot = jnp.where((row % 4).astype(F32) == owners[:, part], 1.0, 0.0).T.astype(BF16)
        arrivals[i].wait()
        if i == 0:
            get_u.wait()
        if i == 1:
            for copy in get_w:
                copy.start()
        for j in range(8):
            cols = slice(256 * j, 256 * j + 256)
            added = jnp.dot(hot, users[:, cols], preferred_element_type=F32)
            x[part, cols] = (x[part, cols].astype(F32) + added).astype(BF16)
        low = jnp.dot(x[part, :], cross_u[...], preferred_element_type=F32)
        left = jnp.concatenate([low.astype(BF16), ones], axis=1)
        if i == 0:
            get_v.wait()
        for j in range(8):
            cols = slice(256 * j, 256 * j + 256)
            cross = jnp.dot(left, cross_v[:, cols], preferred_element_type=F32)
            x[part, cols] = (x[part, cols].astype(F32) * cross).astype(BF16)
    own = x[pl.ds(pl.multiple_of(chip_here * 32, 32), 32), :]
    logits = lax.dot_general(gate_ref[...], own, ROW_BY_ROW, preferred_element_type=F32)
    row = rows((16, 32))
    picked = jnp.where(row // EXPERTS == own_task_ref[...], jax.nn.sigmoid(logits), 0.0)
    gates = picked / jnp.sum(picked, axis=0, keepdims=True)
    row_of = jnp.zeros((1, 128), F32)
    for k in range(EXPERTS):
        gate = widen(jnp.sum(jnp.where(row % EXPERTS == k, gates, 0.0), axis=0, keepdims=True))
        row_of = row_of + (gate if k == 0 else turn(gate, 32 * k))
    gates_ref[...] = row_of
    for copy in get_w:
        copy.wait()
    active = jax.nn.relu(jnp.dot(x[...], w[...], preferred_element_type=F32)).astype(BF16)
    row = rows((16, SLOTS)).astype(F32)
    outs = []
    for k in range(EXPERTS):
        terms = lax.dot_general(heads, active[:, 256 * k : 256 * k + 256], ROW_BY_ROW, preferred_element_type=F32)
        outs.append(jnp.sum(jnp.where(row == tasks * EXPERTS + k, terms, 0.0), axis=0, keepdims=True))
    for b in range(8):
        stack = jnp.concatenate([o[:, 128 * b : 128 * b + 128] for o in outs] + [jnp.zeros((5, 128), F32)], axis=0)
        turns = [stack] + [pltpu.roll(stack, 32 * q, 1) for q in range(1, 4)]
        for q in range(4):
            message = jnp.zeros((1, 128), F32)
            for k in range(EXPERTS):
                message = jnp.where(quarter == k, turns[(k - q) % 4][k : k + 1], message)
            out_ref[4 * b + q : 4 * b + q + 1, :] = message


def home_kernel(got_ref, gates_ref, owner_ref, out_ref):
    total = jnp.sum(got_ref[...], axis=0, keepdims=True) * gates_ref[...]
    total = total + turn(total, 64)
    total = total + turn(total, 32)
    out_ref[...] = jnp.where(owner_ref[...] < REQ_GRP, total[:, 0:32], 0.0)


def body(
    hist, tower_gain, up_w, down_w, query, proj_w, cand, owner, task, cross_u, cross_v, cross_bias, gate_w, expert_w, head_w,
):
    owner, task = owner[None, :], task[None, :]
    everyone = lax.all_gather(cand, CHIPS, axis=0, tiled=True)
    message = pl.pallas_call(
        pack_kernel,
        out_shape=jax.ShapeDtypeStruct((160, 128), BF16),
        in_specs=[VMEM] * 4,
        out_specs=VMEM,
        compiler_params=params(64),
    )(hist.T, tower_gain, query[None, :], head_w.transpose(1, 0, 2))
    pair = lax.all_gather(message, "c", axis=0)
    spread, hist_c, query_c = pl.pallas_call(
        spread_kernel,
        out_shape=(
            jax.ShapeDtypeStruct((N_CHIPS, 72, 128), BF16),
            jax.ShapeDtypeStruct((64, 128), BF16),
            jax.ShapeDtypeStruct((8, 128), F32),
        ),
        in_specs=[VMEM],
        out_specs=(VMEM,) * 3,
        compiler_params=params(63 << 10),
    )(pair)
    tokens = lax.all_to_all(spread, CHIPS, 0, 0, tiled=True)
    swap = lambda x: lax.ppermute(x, "c", [(0, 1), (1, 0)])
    parts = pl.pallas_call(
        tower_kernel,
        out_shape=jax.ShapeDtypeStruct((N_CHIPS, 64, 128), BF16),
        in_specs=[VMEM] * 3 + [HBM] * 2,
        out_specs=VMEM,
        scratch_shapes=[pltpu.VMEM((256, 4096), BF16), pltpu.SemaphoreType.DMA((2,))],
        compiler_params=params(13900),
    )(tokens, up_w, swap(up_w), down_w, swap(down_w))
    summed = lax.all_to_all(parts, CHIPS, 0, 0, tiled=True)
    values = pl.pallas_call(
        values_kernel,
        out_shape=jax.ShapeDtypeStruct((N_CHIPS, 40, 128), BF16),
        in_specs=[VMEM] * 3 + [HBM] * 2,
        out_specs=VMEM,
        scratch_shapes=[pltpu.VMEM((128, 2048), BF16), pltpu.SemaphoreType.DMA((2,))],
        compiler_params=params(12160),
    )(summed, hist_c, query_c, proj_w, swap(proj_w))
    values = lax.all_to_all(values, CHIPS, 0, 0, tiled=True)
    user = pl.pallas_call(
        user_kernel,
        out_shape=jax.ShapeDtypeStruct((128, 128), F32),
        in_specs=[VMEM] * 3,
        out_specs=VMEM,
        compiler_params=params(12288),
    )(values, owner, task)
    users = lax.all_to_all(user, ALL, 0, 0, tiled=True)
    gate_rows = jnp.pad(gate_w.T, ((0, 4), (0, 0)))
    part, gates = pl.pallas_call(
        score_kernel,
        out_shape=(jax.ShapeDtypeStruct((N_CHIPS, 128), F32), jax.ShapeDtypeStruct((1, 128), F32)),
        in_specs=[VMEM, HBM, VMEM, VMEM, HBM, HBM, VMEM, VMEM, HBM, HBM],
        out_specs=(VMEM,) * 2,
        scratch_shapes=[
            pltpu.VMEM((16, 2048), BF16),
            pltpu.VMEM((SLOTS, 2048), BF16),
            pltpu.VMEM((2048, 128), BF16),
            pltpu.VMEM((256, 2048), BF16),
            pltpu.VMEM((2048, 768), BF16),
            pltpu.SemaphoreType.DMA((12,)),
        ],
        compiler_params=params(11700),
    )(users, everyone, task, pair, cross_u, cross_v, cross_bias[None, :], gate_rows, expert_w, swap(expert_w))
    back = lax.all_to_all(part, CHIPS, 0, 0, tiled=True)
    score = pl.pallas_call(
        home_kernel,
        out_shape=jax.ShapeDtypeStruct((1, 32), F32),
        in_specs=[VMEM] * 3,
        out_specs=VMEM,
        compiler_params=params(12288),
    )(back, gates, owner)
    return score[0]


def solution(mesh):
    fine = Mesh(mesh.devices.reshape(mesh.devices.shape[0], 8, 2, 2, 2), ("grp", "z", "xl", "xh", "c"))
    t = ("z", "xl", "xh", "c")
    in_specs = (
        P("grp", t),
        P(None, t),
        P(None, t),
        P(t, None),
        P(t),
        P(t, None),
        P(("grp",) + t, None),
        P(("grp",) + t),
        P(("grp",) + t),
        P(),
        P(),
        P(),
        P(),
        P(None, None, t),
        P(None, None, t),
    )
    return jax.shard_map(body, mesh=fine, in_specs=in_specs, out_specs=P(("grp",) + t), check_vma=False)
```
